32 devices in a mesh: group: 2 (over y), head: 4 (over z), cache: 4 (over x, core).
Axes of the slice: x: 2, y: 2, z: 4, core: 2. Of those that a mesh axis runs over, the one named last changes fastest.
Arguments:
- queries: bfloat16 [512, 4096], P(('group', 'head')), parts along dimension 0, may hold values from -8 to 8
- keys: bfloat16 [256, 128, 4096], P(('group', 'cache'), None, 'head'), parts along dimension 0, may hold values from -8 to 8
- values: bfloat16 [256, 128, 4096], P(('group', 'cache'), None, 'head'), parts along dimension 0, may hold values from -6 to 6
- page_lists: int32 [8, 32], P(('group', 'cache')), parts along dimension 0, may hold values from 0 to 31, as said below
- page_counts: int32 [8], P(('group', 'cache')), parts along dimension 0, may hold values from 1 to 32, as said below
Outputs:
- attended: float32 [512, 4096], P(('group', 'head', 'cache')), parts along dimension 0
- log_sums: float32 [512, 32], P(('group', 'head', 'cache')), parts along dimension 0
The draws below stay inside these ranges and needn't reach their ends.
There are 2 independent parts, one for each index of `group`. The reference program is written for one: setup_inputs(seed, part) draws one part's arguments, and reference() takes and returns one part's arrays. A program takes and returns all parts, laid end to end along the dimension named above; each array names one. Nothing has to cross between parts.
Inputs may be any that keep to these rules, and one draw needn't show every extreme that they name: `page_lists`: row c holds 32 distinct page ids of owner c's pool; only its first page_counts[c] entries are attended. `page_counts`: some owner lists exactly 32 pages in every draw.
All inputs are finite; a program needn't handle non-finite values.
Results may differ from the reference program's by a relative error of at most 0.00038.
Values may be sent and summed in bfloat16 or wider, within the bound.
No kernel may reach another device: no remote copies, remote signals or barrier semaphores. Data moves between devices by JAX's collectives and lax.ppermute only.
A program may use at most 64 MiB of HBM per device.

```python
import math
import jax
import jax.numpy as jnp
from jax import lax

HEADS = 32
DH = 128
PAGE = 128
POOL = 32
MOST = 32
Q_TOK = 256
OWNERS = 4


def page_tables(key):
    base = jax.random.fold_in(key, 101)
    owner_keys = jax.random.split(jax.random.fold_in(base, 1), OWNERS)
    listed = jax.vmap(lambda owner_key: jax.random.permutation(owner_key, POOL)[:MOST])(owner_keys).astype(jnp.int32)
    counts = jax.random.randint(jax.random.fold_in(base, 2), (OWNERS,), 1, MOST // 2 + 1)
    busiest = jax.random.randint(jax.random.fold_in(base, 3), (), 0, OWNERS)
    counts = jnp.where(jnp.arange(OWNERS) == busiest, MOST, counts).astype(jnp.int32)
    return (listed, counts)


def drawn_draw(key, shape):
    return jnp.clip(1.7 * jax.random.normal(key, shape, jnp.float32), -8.0, 8.0)


def draw_page_lists(key, part):
    listed, counts = page_tables(key)
    return listed


def draw_page_counts(key, part):
    listed, counts = page_tables(key)
    return counts


def draw_queries(key, part):
    shape = (Q_TOK, HEADS * DH)
    drawn = drawn_draw(jax.random.fold_in(key, 304), shape)
    return drawn.astype(jnp.bfloat16)


def draw_keys(key, part):
    shape = (OWNERS * POOL, PAGE, HEADS * DH)
    drawn = drawn_draw(jax.random.fold_in(key, 405), shape)
    return drawn.astype(jnp.bfloat16)


def block_levels(stream_key, shape, cuts, smallest, largest):
    factor_of, own = 1.0, jax.random.fold_in(stream_key, 6)
    for position, blocks in cuts:
        steps = jnp.exp(jax.random.uniform(jax.random.fold_in(own, position), (blocks,), jnp.float32, smallest / len(cuts), largest / len(cuts)))
        factor_of = factor_of * jnp.repeat(steps, shape[position] // blocks).reshape([-1 if axis == position else 1 for axis in range(len(shape))])
    return factor_of


def scatter_about(key, dims, scale, most, shards=(), kind=jnp.bfloat16):
    result = scale * jax.random.normal(key, dims, jnp.float32)
    if shards:
        result = result * block_levels(key, dims, shards, -0.22, 0.18)
    return jnp.clip(result, -most, most).astype(kind)


def setup_inputs(seed: int = 0, part: int = 0) -> dict:
    arg_keys = jax.random.split(jax.random.key(seed), 6)
    part_keys = jax.random.split(jax.random.fold_in(arg_keys[5], part), 6)
    queries = draw_queries(jax.random.fold_in(jax.random.fold_in(arg_keys[5], part), 71), part)
    keys = draw_keys(jax.random.fold_in(jax.random.fold_in(arg_keys[5], part), 71), part)
    values = scatter_about(part_keys[2], (OWNERS * POOL, PAGE, HEADS * DH), 1.0, 6.0, ((0, 4), (2, 4)))
    page_lists = draw_page_lists(jax.random.fold_in(jax.random.fold_in(arg_keys[5], part), 71), part)
    page_counts = draw_page_counts(jax.random.fold_in(jax.random.fold_in(arg_keys[5], part), 71), part)
    return {"queries": queries, "keys": keys, "values": values, "page_lists": page_lists, "page_counts": page_counts}


lowest = -1e+30

def reference(queries, keys, values, page_lists, page_counts):
    score_scale = 1.0 / math.sqrt(DH)
    query_heads = queries.reshape(Q_TOK, HEADS, DH).astype(jnp.float32)
    owner_ids = jnp.arange(OWNERS, dtype=jnp.int32)
    page_rows = (owner_ids[:, None] * POOL + page_lists).reshape(-1).astype(jnp.int32)
    live = (jnp.arange(MOST, dtype=jnp.int32)[None, :] < page_counts[:, None]).reshape(-1)

    def update(state, row):
        best, total, accum = state
        key_page = lax.dynamic_index_in_dim(keys, row, 0, keepdims=False).reshape(PAGE, HEADS, DH).astype(jnp.float32)
        value_page = lax.dynamic_index_in_dim(values, row, 0, keepdims=False).reshape(PAGE, HEADS, DH).astype(jnp.float32)
        scores = jnp.einsum('thd,khd->thk', query_heads, key_page) * score_scale
        page_max = lax.optimization_barrier(jnp.max(scores, axis=-1))
        rounded = jnp.exp(scores - page_max[..., None]).astype(jnp.bfloat16)
        weights = lax.optimization_barrier(rounded).astype(jnp.float32)
        page_sum = lax.optimization_barrier(jnp.sum(weights, axis=-1))
        page_out = jnp.einsum('thk,khd->thd', weights, value_page)
        running = jnp.maximum(best, page_max)
        keep = jnp.exp(best - running)
        fresh = jnp.exp(page_max - running)
        return (running, total * keep + fresh * page_sum, accum * keep[..., None] + fresh[..., None] * page_out)

    def visit(state, item):
        row, used = item
        return (lax.cond(used, lambda inner: update(inner, row), lambda inner: inner, state), None)
    start = (jnp.full((Q_TOK, HEADS), lowest, jnp.float32), jnp.zeros((Q_TOK, HEADS), jnp.float32), jnp.zeros((Q_TOK, HEADS, DH), jnp.float32))
    (best, total, accum), _ = lax.scan(visit, start, (page_rows, live))
    attended = (accum / total[..., None]).reshape(Q_TOK, HEADS * DH)
    log_sums = best + jnp.log(total)
    return (attended, log_sums)
```

```python
import functools
import math

import jax
import jax.numpy as jnp
from jax import lax
from jax.experimental import pallas as pl
from jax.experimental.pallas import tpu as pltpu
from jax.sharding import PartitionSpec as P

HEADS = 32
DH = 128
PAGE = 128
LANES = 128
TOK_TILE = 256
VMEM_LIMIT = 50 * 2**20

lowest = -1e30
to_log2 = math.log2(math.e) / math.sqrt(DH)


def attend_kernel(n_parts, *refs):
    count_ref, listed_ref = refs[:2]
    q_refs = refs[2 : 2 + n_parts]
    k_hbm, v_hbm, keep_ref, send_ref = refs[2 + n_parts : 6 + n_parts]
    q_turned, k_pool, v_pool, stats, k_sem, v_sem = refs[6 + n_parts :]
    heads, pool = k_pool.shape[:2]
    all_tok = q_turned.shape[2]
    tile = min(all_tok, TOK_TILE)
    tiles = all_tok // tile
    half = keep_ref.shape[0]
    count = count_ref[0]
    ahead = min(heads, 2)

    def copies(h):
        columns = pl.ds(pl.multiple_of(h * DH, DH), DH)
        return (
            pltpu.make_async_copy(k_hbm.at[:, :, columns], k_pool.at[h], k_sem.at[h]),
            pltpu.make_async_copy(v_hbm.at[:, :, columns], v_pool.at[h], v_sem.at[h]),
        )

    for h in range(ahead):
        for copy in copies(h):
            copy.start()
    row = 0
    for q_ref in q_refs:
        rows = q_ref.shape[0]
        for h in range(heads):
            q_turned[h, :, row : row + rows] = q_ref[:, h * DH : (h + 1) * DH].T
        row += rows
    stats[...] = jnp.zeros_like(stats)
    ones = jnp.ones((8, PAGE), jnp.bfloat16)

    def unit(u, carry):
        h, t = u // tiles, lax.rem(u, tiles)

        @pl.when(t == 0)
        def _():
            for copy in copies(h):
                copy.wait()

            @pl.when(h + ahead < heads)
            def _():
                for copy in copies(h + ahead):
                    copy.start()

        start = pl.multiple_of(t * tile, tile)
        columns = pl.ds(start, tile)
        q_tile = q_turned[h, :, columns]
        scores, tops = [], []
        for i in range(pool):
            s = jnp.dot(k_pool[h, listed_ref[0, i]], q_tile, preferred_element_type=jnp.float32)
            scores.append(s)
            tops.append(jnp.max(s, axis=0, keepdims=True))
        used = [jnp.where(i < count, tops[i], lowest) for i in range(pool)]
        best = functools.reduce(jnp.maximum, used)
        total, accum = 0.0, 0.0
        for i in range(pool):
            weights = jnp.exp2((scores[i] - tops[i]) * to_log2).astype(jnp.bfloat16)
            turned = v_pool[h, listed_ref[0, i]].T
            page_out = jnp.dot(
                jnp.concatenate([turned, ones], axis=0),
                weights,
                preferred_element_type=jnp.float32,
            )
            fresh = jnp.exp2((used[i] - best) * to_log2)
            total = total + fresh * page_out[DH : DH + 1]
            accum = accum + fresh * page_out[:DH]
        out = (accum / total).T
        stats[pl.ds(h, 1), columns] = best * to_log2 + jnp.log2(total)
        lanes = pl.ds(pl.multiple_of(h * DH, DH), DH)
        if tiles == 1:
            keep_ref[:, lanes] = out[:half]
            send_ref[:, lanes] = out[half:]
        else:

            @pl.when(start < half)
            def _():
                keep_ref[columns, lanes] = out

            @pl.when(start >= half)
            def _():
                send_ref[pl.ds(pl.multiple_of(start - half, tile), tile), lanes] = out

        return carry

    lax.fori_loop(0, heads * tiles, unit, 0)
    for t in range(tiles):
        turned = stats[:, t * tile : (t + 1) * tile].T
        for r in range(0, tile, 8):
            row = t * tile + r
            ref = keep_ref if row < half else send_ref
            row = row if row < half else row - half
            ref[row : row + 8, heads * DH :] = turned[r : r + 8]


def attend(q_parts, keys, values, page_lists, page_counts):
    all_tok = sum(part.shape[0] for part in q_parts)
    pool = keys.shape[0]
    heads = keys.shape[2] // DH
    in_vmem = pl.BlockSpec(memory_space=pltpu.VMEM)
    in_smem = pl.BlockSpec(memory_space=pltpu.SMEM)
    anywhere = pl.BlockSpec(memory_space=pl.ANY)
    out = jax.ShapeDtypeStruct((all_tok // 2, heads * DH + LANES), jnp.float32)
    return pl.pallas_call(
        functools.partial(attend_kernel, len(q_parts)),
        in_specs=[in_smem, in_smem] + [in_vmem] * len(q_parts) + [anywhere, anywhere],
        out_specs=[in_vmem, in_vmem],
        scratch_shapes=[
            pltpu.VMEM((heads, DH, all_tok), jnp.bfloat16),
            pltpu.VMEM((heads, pool, PAGE, DH), jnp.bfloat16),
            pltpu.VMEM((heads, pool, PAGE, DH), jnp.bfloat16),
            pltpu.VMEM((LANES, all_tok), jnp.float32),
            pltpu.SemaphoreType.DMA((heads,)),
            pltpu.SemaphoreType.DMA((heads,)),
        ],
        out_shape=[out, out],
        compiler_params=pltpu.CompilerParams(vmem_limit_bytes=VMEM_LIMIT),
        name="attend",
    )(page_counts, page_lists, *q_parts, keys, values)


def merge_kernel(heads, mine_ref, theirs_ref, *out_refs):
    rows = out_refs[0].shape[0]
    for i, out_ref in enumerate(out_refs):
        part = slice(i * rows, (i + 1) * rows)
        logs = []
        for h in range(heads):
            lanes = slice(h * DH, (h + 1) * DH)
            stat = slice(heads * DH + h, heads * DH + h + 1)
            first, second = mine_ref[part, stat], theirs_ref[part, stat]
            top = jnp.maximum(first, second)
            a, b = jnp.exp2(first - top), jnp.exp2(second - top)
            both = a + b
            out_ref[:, lanes] = (mine_ref[part, lanes] * a + theirs_ref[part, lanes] * b) / both
        first, second = mine_ref[part, heads * DH :], theirs_ref[part, heads * DH :]
        top = jnp.maximum(first, second)
        both = jnp.exp2(first - top) + jnp.exp2(second - top)
        out_ref[:, heads * DH :] = top + jnp.log2(both)


def merge(mine, theirs, heads, n_out):
    out = jax.ShapeDtypeStruct((mine.shape[0] // n_out, mine.shape[1]), jnp.float32)
    return pl.pallas_call(
        functools.partial(merge_kernel, heads),
        out_shape=[out] * n_out,
        compiler_params=pltpu.CompilerParams(vmem_limit_bytes=VMEM_LIMIT),
        name="merge",
    )(mine, theirs)


def across(value, axis, size, bit):
    return lax.ppermute(value, axis, [(i, i ^ bit) for i in range(size)])


def on_device(queries, keys, values, page_lists, page_counts):
    n_head = lax.axis_size("head")
    n_cache = lax.axis_size("cache")
    tok_local = queries.shape[0]
    heads = keys.shape[2] // DH
    share = tok_local // n_cache
    bits = [1 << i for i in range(n_cache.bit_length() - 1)]
    mine = lax.dynamic_slice_in_dim(queries, lax.axis_index("cache") * share, share, 0)
    part = lax.all_to_all(
        mine.reshape(share, n_head, heads * DH), "head", split_axis=1, concat_axis=0, tiled=True
    ).reshape(n_head * share, heads * DH)
    parts = [part]
    for bit in reversed(bits):
        parts = parts + [across(part, "cache", n_cache, bit) for part in parts]
    keep, send = attend(parts, keys, values, page_lists, page_counts)
    for bit in bits:
        theirs = across(send, "cache", n_cache, bit)
        if bit != bits[-1]:
            keep, send = merge(keep, theirs, heads, 2)
        else:
            (keep,) = merge(keep, theirs, heads, 1)
    result = lax.all_to_all(
        keep.reshape(n_head, share, keep.shape[1]), "head", split_axis=0, concat_axis=0, tiled=True
    )
    attended = result[:, :, : heads * DH].transpose(1, 0, 2).reshape(share, HEADS * DH)
    logged = result[:, :, heads * DH : heads * DH + heads].transpose(1, 0, 2)
    return attended, logged.reshape(share, HEADS) * math.log(2.0)


def solution(mesh):
    in_specs = (
        P(("group", "head"), None),
        P(("group", "cache"), None, "head"),
        P(("group", "cache"), None, "head"),
        P(("group", "cache"), None),
        P(("group", "cache")),
    )
    out_specs = (P(("group", "head", "cache"), None), P(("group", "head", "cache"), None))
    return jax.shard_map(
        on_device, mesh=mesh, in_specs=in_specs, out_specs=out_specs, check_vma=False
    )
```

```python
import functools
import math

import jax
import jax.numpy as jnp
from jax import lax
from jax.experimental import pallas as pl
from jax.experimental.pallas import tpu as pltpu
from jax.sharding import PartitionSpec as P

HEADS = 32
DH = 128
PAGE = 128
LANES = 128
TOK_TILE = 256
GROUP = 2
MOST_PERMUTES = 8
VMEM_LIMIT = 50 * 2**20

lowest = -1e30
to_log2 = math.log2(math.e) / math.sqrt(DH)


def attend_kernel(n_parts, limits_ref, *refs):
    q_refs = refs[:n_parts]
    k_hbm, v_hbm, keep_ref, send_ref = refs[n_parts : n_parts + 4]
    q_turned, k_pool, v_pool, stats, k_sem, v_sem = refs[n_parts + 4 :]
    heads, pool = k_pool.shape[:2]
    all_tok = q_turned.shape[2]
    tile = min(all_tok, TOK_TILE)
    tiles = all_tok // tile
    half = keep_ref.shape[0]
    ahead = min(heads, 2)

    def copies(h):
        columns = pl.ds(pl.multiple_of(h * DH, DH), DH)
        return (
            pltpu.make_async_copy(k_hbm.at[:, :, columns], k_pool.at[h], k_sem.at[h]),
            pltpu.make_async_copy(v_hbm.at[:, :, columns], v_pool.at[h], v_sem.at[h]),
        )

    for h in range(ahead):
        for copy in copies(h):
            copy.start()
    for h in range(heads):
        rows = [q_ref[:, h * DH : (h + 1) * DH] for q_ref in q_refs]
        q_turned[h] = jnp.concatenate(rows, axis=0).T
    stats[...] = jnp.zeros_like(stats)
    ones = jnp.ones((8, PAGE), jnp.bfloat16)

    def unit(u, carry):
        h, t = u // tiles, lax.rem(u, tiles)

        @pl.when(t == 0)
        def _():
            for copy in copies(h):
                copy.wait()

            @pl.when(h + ahead < heads)
            def _():
                for copy in copies(h + ahead):
                    copy.start()

        start = pl.multiple_of(t * tile, tile)
        columns = pl.ds(start, tile)
        q_tile = q_turned[h, :, columns]
        scores, tops = [], []
        for i in range(0, pool, GROUP):
            block = k_pool[h, i : i + GROUP].reshape(GROUP * PAGE, DH)
            both = jnp.dot(block, q_tile, preferred_element_type=jnp.float32)
            for j in range(GROUP):
                scores.append(both[j * PAGE : (j + 1) * PAGE])
                tops.append(jnp.max(scores[-1], axis=0, keepdims=True))
        used = [jnp.minimum(tops[i], limits_ref[i : i + 1, :]) for i in range(pool)]
        best = functools.reduce(jnp.maximum, used)
        total, accum = 0.0, 0.0
        for i in range(pool):
            weights = jnp.exp2((scores[i] - tops[i]) * to_log2).astype(jnp.bfloat16)
            page_out = jnp.dot(
                jnp.concatenate([v_pool[h, i].T, ones], axis=0),
                weights,
                preferred_element_type=jnp.float32,
            )
            fresh = jnp.exp2((used[i] - best) * to_log2)
            total = total + fresh * page_out[DH : DH + 1]
            accum = accum + fresh * page_out[:DH]
        out = (accum / total).T
        stats[pl.ds(h, 1), columns] = best * to_log2 + jnp.log2(total)
        lanes = pl.ds(pl.multiple_of(h * DH, DH), DH)
        if tiles == 1:
            keep_ref[:, lanes] = out[:half]
            send_ref[:, lanes] = out[half:]
        else:

            @pl.when(start < half)
            def _():
                keep_ref[columns, lanes] = out

            @pl.when(start >= half)
            def _():
                send_ref[pl.ds(pl.multiple_of(start - half, tile), tile), lanes] = out

        return carry

    lax.fori_loop(0, heads * tiles, unit, 0)
    for t in range(tiles):
        turned = stats[:, t * tile : (t + 1) * tile].T
        for r in range(0, tile, 8):
            row = t * tile + r
            ref = keep_ref if row < half else send_ref
            row = row if row < half else row - half
            ref[row : row + 8, heads * DH :] = turned[r : r + 8]


def attend(q_parts, keys, values, limits):
    all_tok = sum(part.shape[0] for part in q_parts)
    pool = keys.shape[0]
    heads = keys.shape[2] // DH
    in_vmem = pl.BlockSpec(memory_space=pltpu.VMEM)
    anywhere = pl.BlockSpec(memory_space=pl.ANY)
    out = jax.ShapeDtypeStruct((all_tok // 2, heads * DH + LANES), jnp.float32)
    return pl.pallas_call(
        functools.partial(attend_kernel, len(q_parts)),
        in_specs=[in_vmem] * (1 + len(q_parts)) + [anywhere, anywhere],
        out_specs=[in_vmem, in_vmem],
        scratch_shapes=[
            pltpu.VMEM((heads, DH, all_tok), jnp.bfloat16),
            pltpu.VMEM((heads, pool, PAGE, DH), jnp.bfloat16),
            pltpu.VMEM((heads, pool, PAGE, DH), jnp.bfloat16),
            pltpu.VMEM((LANES, all_tok), jnp.float32),
            pltpu.SemaphoreType.DMA((heads,)),
            pltpu.SemaphoreType.DMA((heads,)),
        ],
        out_shape=[out, out],
        compiler_params=pltpu.CompilerParams(vmem_limit_bytes=VMEM_LIMIT),
        name="attend",
    )(limits, *q_parts, keys, values)


def rounded(x):
    return jnp.where(x < 0, x - 0.5, x + 0.5).astype(jnp.int32)


def encode(outs, logs, out_ref):
    heads = len(outs)
    where = (slice(None),) * (len(out_ref.shape) - 1)
    powers = []
    for h, out in enumerate(outs):
        largest = jnp.max(jnp.abs(out), axis=-1, keepdims=True)
        power = jnp.ceil(jnp.log2(jnp.maximum(largest, 2.0**-100)))
        powers.append(power)
        out_ref[where + (slice(h * DH, (h + 1) * DH),)] = rounded(
            out * (jnp.exp2(-power) * 32767.0)
        ).astype(jnp.int16)
    fixed = rounded(logs * 2.0**19)
    high = lax.shift_right_arithmetic(fixed, 16)
    low = lax.bitwise_and(fixed, 65535) - 32768
    pad = jnp.zeros(logs.shape[:-1] + (LANES - 3 * heads,), jnp.int32)
    stat = jnp.concatenate(
        [high[..., :heads], low[..., :heads]] + [p.astype(jnp.int32) for p in powers] + [pad], axis=-1
    )
    out_ref[where + (slice(heads * DH, heads * DH + LANES),)] = stat.astype(jnp.int16)


def decode(heads, ref):
    where = (slice(None),) * (len(ref.shape) - 1)
    stat = ref[where + (slice(heads * DH, heads * DH + LANES),)].astype(jnp.int32)
    fixed = lax.shift_left(stat[..., :heads], 16) + (stat[..., heads : 2 * heads] + 32768)
    logs = fixed.astype(jnp.float32) * 2.0**-19
    steps = jnp.exp2(stat[..., 2 * heads : 3 * heads].astype(jnp.float32)) * (1.0 / 32767.0)
    outs = []
    for h in range(heads):
        coded = ref[where + (slice(h * DH, (h + 1) * DH),)].astype(jnp.int32).astype(jnp.float32)
        outs.append(coded * steps[..., h : h + 1])
    return outs, logs


def plain(heads, ref):
    where = (slice(None),) * (len(ref.shape) - 1)
    outs = [ref[where + (slice(h * DH, (h + 1) * DH),)] for h in range(heads)]
    return outs, ref[where + (slice(heads * DH, heads * DH + heads),)]


def merge_kernel(heads, last, mine_ref, theirs_ref, *out_refs):
    mine, mine_logs = plain(heads, mine_ref)
    theirs, their_logs = (decode if theirs_ref.dtype == jnp.int16 else plain)(heads, theirs_ref)
    top = jnp.maximum(mine_logs, their_logs)
    first, second = jnp.exp2(mine_logs - top), jnp.exp2(their_logs - top)
    both = first + second
    first, second, logs = first / both, second / both, top + jnp.log2(both)
    outs = [
        mine[h] * first[..., h : h + 1] + theirs[h] * second[..., h : h + 1] for h in range(heads)
    ]
    if last:
        if len(out_refs) == 1:
            encode(outs, logs, out_refs[0])
        else:
            for block, out_ref in enumerate(out_refs):
                encode([out[block] for out in outs], logs[block], out_ref)
    else:
        keep_ref, send_ref = out_refs
        half = keep_ref.shape[1]
        for h in range(heads):
            keep_ref[:, :, h * DH : (h + 1) * DH] = outs[h][:, :half]
        pad = jnp.zeros(logs.shape[:-1] + (LANES - heads,), jnp.float32)
        keep_ref[:, :, heads * DH :] = jnp.concatenate([logs, pad], axis=-1)[:, :half]
        encode([out[:, half:] for out in outs], logs[:, half:], send_ref)


def merge(mine, theirs, heads, out_shapes, last):
    return pl.pallas_call(
        functools.partial(merge_kernel, heads, last),
        out_shape=out_shapes,
        compiler_params=pltpu.CompilerParams(vmem_limit_bytes=VMEM_LIMIT),
        name="merge",
    )(mine, theirs)


def place_kernel(heads, axis, *refs):
    part_refs, (out_ref, logs_ref) = refs[:-2], refs[-2:]
    here = lax.axis_index(axis) if len(part_refs) > 1 else 0
    pieces = []
    if len(part_refs) > 1:
        for k, part_ref in enumerate(part_refs):
            outs, logs = decode(heads, part_ref)
            at = lax.bitwise_xor(here, k)
            out_ref[:, pl.ds(pl.multiple_of(at * heads * DH, DH), heads * DH)] = jnp.concatenate(
                outs, axis=-1
            )
            pieces.append((at, logs))
        columns = []
        for z in range(len(part_refs)):
            columns.append(sum(jnp.where(at == z, logs, 0.0) for at, logs in pieces))
    else:
        outs, logs = decode(heads, part_refs[0])
        for z in range(logs.shape[0]):
            for h in range(heads):
                first = (z * heads + h) * DH
                out_ref[:, first : first + DH] = outs[h][z]
        columns = [logs[z] for z in range(logs.shape[0])]
    logs_ref[...] = jnp.concatenate(columns, axis=-1) * math.log(2.0)


def place(parts, heads, axis, share):
    return pl.pallas_call(
        functools.partial(place_kernel, heads, axis),
        out_shape=[
            jax.ShapeDtypeStruct((share, HEADS * DH), jnp.float32),
            jax.ShapeDtypeStruct((share, HEADS), jnp.float32),
        ],
        compiler_params=pltpu.CompilerParams(vmem_limit_bytes=VMEM_LIMIT),
        name="place",
    )(*parts)


def across(value, axis, size, bit):
    return lax.ppermute(value, axis, [(i, i ^ bit) for i in range(size)])


def page_limits(page_lists, page_counts, pool, width):
    slots = jnp.arange(page_lists.shape[1], dtype=jnp.int32)
    pages = jnp.arange(pool, dtype=jnp.int32)
    live = jnp.any(
        (page_lists[0][None, :] == pages[:, None]) & (slots < page_counts[0])[None, :], axis=1
    )
    return jnp.broadcast_to(jnp.where(live, -lowest, lowest)[:, None], (pool, width))


def on_device(queries, keys, values, page_lists, page_counts):
    n_head = lax.axis_size("head")
    n_cache = lax.axis_size("cache")
    heads = keys.shape[2] // DH
    share = queries.shape[0] // n_cache
    bits = [1 << i for i in range(n_cache.bit_length() - 1)]
    direct = n_head <= MOST_PERMUTES
    head_at, cache_at = lax.axis_index("head"), lax.axis_index("cache")
    order = [0]
    for bit in reversed(bits):
        order = order + [share_at ^ bit for share_at in order]
    shares = queries.reshape(n_cache, share, n_head, heads * DH)

    def pick(names):
        return jnp.concatenate(
            [lax.dynamic_index_in_dim(shares, cache_at ^ name, 0, keepdims=False) for name in names]
        )

    same = pick(order[: n_cache // 2])
    rows = same.shape[0]

    def for_head(part, k):
        return lax.dynamic_index_in_dim(part, head_at ^ k, 1, keepdims=False)

    if direct:
        parts = [across(for_head(same, k), "head", n_head, k) for k in range(1, n_head)]
        swapped = [across(part, "cache", n_cache, 1) for part in parts]
        other = pick(order[n_cache // 2 :])
        q_parts = [for_head(same, 0)] + parts + [for_head(other, 0)] + swapped
    else:
        moved = lax.all_to_all(same, "head", split_axis=1, concat_axis=0, tiled=True)
        moved = moved.reshape(n_head * rows, heads * DH)
        q_parts = [moved, across(moved, "cache", n_cache, 1)]
    all_tok = n_head * queries.shape[0]
    limits = page_limits(page_lists, page_counts, keys.shape[0], min(all_tok, TOK_TILE))
    keep, send = attend(q_parts, keys, values, limits)
    width = keep.shape[1]
    keep = keep.reshape(n_head, rows, width)
    send = send.reshape(n_head, rows, width)
    for bit in bits:
        theirs = across(send, "cache", n_cache, bit)
        if bit != bits[-1]:
            half = keep.shape[1] // 2
            shapes = [
                jax.ShapeDtypeStruct((n_head, half, width), jnp.float32),
                jax.ShapeDtypeStruct((n_head, half, width), jnp.int16),
            ]
            keep, send = merge(keep, theirs, heads, shapes, False)
        elif direct:
            shapes = [jax.ShapeDtypeStruct((share, width), jnp.int16)] * n_head
            blocks = merge(keep, theirs, heads, shapes, True)
            parts = [blocks[0]] + [across(blocks[k], "head", n_head, k) for k in range(1, n_head)]
        else:
            shapes = [jax.ShapeDtypeStruct((n_head, share, width), jnp.int16)]
            (blocks,) = merge(keep, theirs, heads, shapes, True)
            parts = [lax.all_to_all(blocks, "head", split_axis=0, concat_axis=0, tiled=True)]
    return tuple(place(parts, heads, "head", share))


def solution(mesh):
    in_specs = (
        P(("group", "head"), None),
        P(("group", "cache"), None, "head"),
        P(("group", "cache"), None, "head"),
        P(("group", "cache"), None),
        P(("group", "cache")),
    )
    out_specs = (P(("group", "head", "cache"), None), P(("group", "head", "cache"), None))
    return jax.shard_map(
        on_device, mesh=mesh, in_specs=in_specs, out_specs=out_specs, check_vma=False
    )
```

```python
import functools
import math

import jax
import jax.numpy as jnp
from jax import lax
from jax.experimental import pallas as pl
from jax.experimental.pallas import tpu as pltpu
from jax.sharding import PartitionSpec as P

HEADS = 32
DH = 128
PAGE = 128
LANES = 128
TOK_TILE = 256
GROUP = 4
MOST_PERMUTES = 8
VMEM_LIMIT = 50 * 2**20

lowest = -1e30
to_log2 = math.log2(math.e) / math.sqrt(DH)


def attend_kernel(n_parts, starts, limits_ref, *refs):
    q_refs = refs[:n_parts]
    k_hbm, v_hbm, k_first, v_first = refs[n_parts : n_parts + 4]
    out_refs = refs[n_parts + 4 : n_parts + 4 + len(starts)]
    q_turned, k_pool, v_pool, stats, k_sem, v_sem = refs[n_parts + 4 + len(starts) :]
    heads, pool = k_pool.shape[:2]
    all_tok = q_turned.shape[2]
    tile = min(all_tok, TOK_TILE)
    tiles = all_tok // tile
    ahead = min(heads, 3)

    def copies(h):
        columns = pl.ds(pl.multiple_of(h * DH, DH), DH)
        return (
            pltpu.make_async_copy(k_hbm.at[:, :, columns], k_pool.at[h], k_sem.at[h]),
            pltpu.make_async_copy(v_hbm.at[:, :, columns], v_pool.at[h], v_sem.at[h]),
        )

    for h in range(1, ahead):
        for copy in copies(h):
            copy.start()
    k_pool[0] = k_first[...]
    v_pool[0] = v_first[...]
    for h in range(heads):
        rows = [q_ref[:, h * DH : (h + 1) * DH] for q_ref in q_refs]
        q_turned[h] = jnp.concatenate(rows, axis=0).T
    stats[...] = jnp.zeros_like(stats)
    ones = jnp.ones((8, PAGE), jnp.bfloat16)

    def unit(u, carry):
        h, t = u // tiles, lax.rem(u, tiles)

        @pl.when(t == 0)
        def _():
            @pl.when(h > 0)
            def _():
                for copy in copies(h):
                    copy.wait()

            @pl.when(h + ahead < heads)
            def _():
                for copy in copies(h + ahead):
                    copy.start()

        start = pl.multiple_of(t * tile, tile)
        columns = pl.ds(start, tile)
        q_tile = q_turned[h, :, columns]
        scores, tops = [], []
        for i in range(0, pool, GROUP):
            block = k_pool[h, i : i + GROUP].reshape(GROUP * PAGE, DH)
            both = jnp.dot(block, q_tile, preferred_element_type=jnp.float32)
            for j in range(GROUP):
                scores.append(both[j * PAGE : (j + 1) * PAGE])
                tops.append(jnp.max(scores[-1], axis=0, keepdims=True))
        used = [jnp.minimum(tops[i], limits_ref[i : i + 1, :]) for i in range(pool)]
        best = functools.reduce(jnp.maximum, used)
        total, accum = 0.0, 0.0
        for i in range(pool):
            weights = jnp.exp2((scores[i] - tops[i]) * to_log2).astype(jnp.bfloat16)
            page_out = jnp.dot(
                jnp.concatenate([v_pool[h, i].T, ones], axis=0),
                weights,
                preferred_element_type=jnp.float32,
            )
            fresh = jnp.exp2((used[i] - best) * to_log2)
            total = total + fresh * page_out[DH : DH + 1]
            accum = accum + fresh * page_out[:DH]
        out = (accum / total).T
        stats[pl.ds(h, 1), columns] = best * to_log2 + jnp.log2(total)
        lanes = pl.ds(pl.multiple_of(h * DH, DH), DH)
        for first, out_ref in zip(starts, out_refs):
            length = out_ref.shape[0]
            if tiles == 1:
                out_ref[:, lanes] = out[first : first + length]
            else:

                @pl.when((start >= first) & (start < first + length))
                def _():
                    out_ref[pl.ds(pl.multiple_of(start - first, tile), tile), lanes] = out

        return carry

    lax.fori_loop(0, heads * tiles, unit, 0)
    for t in range(tiles):
        turned = stats[:, t * tile : (t + 1) * tile].T
        for first, out_ref in zip(starts, out_refs):
            low = max(first, t * tile)
            high = min(first + out_ref.shape[0], (t + 1) * tile)
            if low < high:
                out_ref[low - first : high - first, heads * DH :] = turned[
                    low - t * tile : high - t * tile
                ]


def attend(q_parts, keys, values, limits, starts):
    all_tok = sum(part.shape[0] for part in q_parts)
    pool = keys.shape[0]
    heads = keys.shape[2] // DH
    in_vmem = pl.BlockSpec(memory_space=pltpu.VMEM)
    anywhere = pl.BlockSpec(memory_space=pl.ANY)
    outs = [
        jax.ShapeDtypeStruct((end - first, heads * DH + LANES), jnp.float32)
        for first, end in zip(starts, starts[1:] + [all_tok])
    ]
    return pl.pallas_call(
        functools.partial(attend_kernel, len(q_parts), starts),
        in_specs=[in_vmem] * (1 + len(q_parts)) + [anywhere, anywhere, in_vmem, in_vmem],
        out_specs=[in_vmem] * len(outs),
        scratch_shapes=[
            pltpu.VMEM((heads, DH, all_tok), jnp.bfloat16),
            pltpu.VMEM((heads, pool, PAGE, DH), jnp.bfloat16),
            pltpu.VMEM((heads, pool, PAGE, DH), jnp.bfloat16),
            pltpu.VMEM((LANES, all_tok), jnp.float32),
            pltpu.SemaphoreType.DMA((heads,)),
            pltpu.SemaphoreType.DMA((heads,)),
        ],
        out_shape=outs,
        compiler_params=pltpu.CompilerParams(vmem_limit_bytes=VMEM_LIMIT),
        name="attend",
    )(limits, *q_parts, keys, values, keys[:, :, :DH], values[:, :, :DH])


def rounded(x):
    return jnp.where(x < 0, x - 0.5, x + 0.5).astype(jnp.int32)


def encode(outs, logs, out_ref):
    heads = len(outs)
    where = (slice(None),) * (len(out_ref.shape) - 1)
    powers = []
    for h, out in enumerate(outs):
        largest = jnp.max(jnp.abs(out), axis=-1, keepdims=True)
        power = jnp.ceil(jnp.log2(jnp.maximum(largest, 2.0**-100)))
        powers.append(power)
        out_ref[where + (slice(h * DH, (h + 1) * DH),)] = rounded(
            out * (jnp.exp2(-power) * 32767.0)
        ).astype(jnp.int16)
    fixed = rounded(logs * 2.0**19)
    high = lax.shift_right_arithmetic(fixed, 16)
    low = lax.bitwise_and(fixed, 65535) - 32768
    pad = jnp.zeros(logs.shape[:-1] + (LANES - 3 * heads,), jnp.int32)
    stat = jnp.concatenate(
        [high[..., :heads], low[..., :heads]] + [p.astype(jnp.int32) for p in powers] + [pad], axis=-1
    )
    out_ref[where + (slice(heads * DH, heads * DH + LANES),)] = stat.astype(jnp.int16)


def decode(heads, ref):
    where = (slice(None),) * (len(ref.shape) - 1)
    stat = ref[where + (slice(heads * DH, heads * DH + LANES),)].astype(jnp.int32)
    fixed = lax.shift_left(stat[..., :heads], 16) + (stat[..., heads : 2 * heads] + 32768)
    logs = fixed.astype(jnp.float32) * 2.0**-19
    steps = jnp.exp2(stat[..., 2 * heads : 3 * heads].astype(jnp.float32)) * (1.0 / 32767.0)
    outs = []
    for h in range(heads):
        coded = ref[where + (slice(h * DH, (h + 1) * DH),)].astype(jnp.int32).astype(jnp.float32)
        outs.append(coded * steps[..., h : h + 1])
    return outs, logs


def plain(heads, ref):
    where = (slice(None),) * (len(ref.shape) - 1)
    outs = [ref[where + (slice(h * DH, (h + 1) * DH),)] for h in range(heads)]
    return outs, ref[where + (slice(heads * DH, heads * DH + heads),)]


def merge_kernel(heads, last, mine_ref, theirs_ref, *out_refs):
    mine, mine_logs = plain(heads, mine_ref)
    theirs, their_logs = (decode if theirs_ref.dtype == jnp.int16 else plain)(heads, theirs_ref)
    top = jnp.maximum(mine_logs, their_logs)
    first, second = jnp.exp2(mine_logs - top), jnp.exp2(their_logs - top)
    both = first + second
    first, second, logs = first / both, second / both, top + jnp.log2(both)
    outs = [
        mine[h] * first[..., h : h + 1] + theirs[h] * second[..., h : h + 1] for h in range(heads)
    ]
    if last:
        if len(out_refs) == 1:
            encode(outs, logs, out_refs[0])
        else:
            for block, out_ref in enumerate(out_refs):
                encode([out[block] for out in outs], logs[block], out_ref)
    else:
        keep_ref, send_ref = out_refs
        half = keep_ref.shape[1]
        for h in range(heads):
            keep_ref[:, :, h * DH : (h + 1) * DH] = outs[h][:, :half]
        pad = jnp.zeros(logs.shape[:-1] + (LANES - heads,), jnp.float32)
        keep_ref[:, :, heads * DH :] = jnp.concatenate([logs, pad], axis=-1)[:, :half]
        encode([out[:, half:] for out in outs], logs[:, half:], send_ref)


def merge(mine, theirs, heads, out_shapes, last):
    return pl.pallas_call(
        functools.partial(merge_kernel, heads, last),
        out_shape=out_shapes,
        compiler_params=pltpu.CompilerParams(vmem_limit_bytes=VMEM_LIMIT),
        name="merge",
    )(mine, theirs)


def place_kernel(heads, axis, *refs):
    part_refs, (out_ref, logs_ref) = refs[:-2], refs[-2:]
    here = lax.axis_index(axis) if len(part_refs) > 1 else 0
    pieces = []
    if len(part_refs) > 1:
        for k, part_ref in enumerate(part_refs):
            outs, logs = decode(heads, part_ref)
            at = lax.bitwise_xor(here, k)
            out_ref[:, pl.ds(pl.multiple_of(at * heads * DH, DH), heads * DH)] = jnp.concatenate(
                outs, axis=-1
            )
            pieces.append((at, logs))
        columns = []
        for z in range(len(part_refs)):
            columns.append(sum(jnp.where(at == z, logs, 0.0) for at, logs in pieces))
    else:
        outs, logs = decode(heads, part_refs[0])
        for z in range(logs.shape[0]):
            for h in range(heads):
                first = (z * heads + h) * DH
                out_ref[:, first : first + DH] = outs[h][z]
        columns = [logs[z] for z in range(logs.shape[0])]
    logs_ref[...] = jnp.concatenate(columns, axis=-1) * math.log(2.0)


def place(parts, heads, axis, share):
    return pl.pallas_call(
        functools.partial(place_kernel, heads, axis),
        out_shape=[
            jax.ShapeDtypeStruct((share, HEADS * DH), jnp.float32),
            jax.ShapeDtypeStruct((share, HEADS), jnp.float32),
        ],
        compiler_params=pltpu.CompilerParams(vmem_limit_bytes=VMEM_LIMIT),
        name="place",
    )(*parts)


def across(value, axis, size, bit):
    return lax.ppermute(value, axis, [(i, i ^ bit) for i in range(size)])


def page_limits(page_lists, page_counts, pool, width):
    slots = jnp.arange(page_lists.shape[1], dtype=jnp.int32)
    pages = jnp.arange(pool, dtype=jnp.int32)
    live = jnp.any(
        (page_lists[0][None, :] == pages[:, None]) & (slots < page_counts[0])[None, :], axis=1
    )
    return jnp.broadcast_to(jnp.where(live, -lowest, lowest)[:, None], (pool, width))


def on_device(queries, keys, values, page_lists, page_counts):
    n_head = lax.axis_size("head")
    n_cache = lax.axis_size("cache")
    heads = keys.shape[2] // DH
    share = queries.shape[0] // n_cache
    bits = [1 << i for i in range(n_cache.bit_length() - 1)]
    direct = n_head <= MOST_PERMUTES
    head_at, cache_at = lax.axis_index("head"), lax.axis_index("cache")
    order = [0]
    for bit in reversed(bits):
        order = order + [share_at ^ bit for share_at in order]

    def pick(names, k):
        width = heads * DH
        at = (head_at ^ k) * width
        pieces = [
            lax.dynamic_slice(queries, ((cache_at ^ name) * share, at), (share, width))
            for name in names
        ]
        return jnp.concatenate(pieces)

    half = n_cache // 2
    rows = half * share
    if direct:
        parts = [across(pick(order[:half], k), "head", n_head, k) for k in range(1, n_head)]
        swapped = [across(part, "cache", n_cache, 1) for part in parts]
        q_parts = [pick(order[:half], 0)] + parts + [pick(order[half:], 0)] + swapped
    else:
        shares = queries.reshape(n_cache, share, HEADS * DH)
        same = jnp.concatenate(
            [lax.dynamic_index_in_dim(shares, cache_at ^ name, 0, False) for name in order[:half]]
        )
        moved = lax.all_to_all(
            same.reshape(rows, n_head, heads * DH), "head", split_axis=1, concat_axis=0, tiled=True
        ).reshape(n_head * rows, heads * DH)
        q_parts = [moved, across(moved, "cache", n_cache, 1)]
    all_tok = n_head * queries.shape[0]
    limits = page_limits(page_lists, page_counts, keys.shape[0], min(all_tok, TOK_TILE))
    groups = [range(n_head // 2), range(n_head // 2, n_head)] if direct else [range(n_head)]
    starts = [group[0] * rows for group in groups]
    starts = starts + [n_head * rows + first for first in starts]
    states = attend(q_parts, keys, values, limits, starts)
    width = states[0].shape[1]
    states = [state.reshape(-1, rows, width) for state in states]
    states = list(zip(states[: len(groups)], states[len(groups) :]))[::-1]
    groups = groups[::-1]
    parts = [None] * n_head
    for bit in bits:
        arrived = [across(send, "cache", n_cache, bit) for _, send in states]
        for g, (keep, _) in enumerate(states):
            size, length, _ = keep.shape
            if bit != bits[-1]:
                shapes = [
                    jax.ShapeDtypeStruct((size, length // 2, width), jnp.float32),
                    jax.ShapeDtypeStruct((size, length // 2, width), jnp.int16),
                ]
                states[g] = merge(keep, arrived[g], heads, shapes, False)
            elif direct:
                shapes = [jax.ShapeDtypeStruct((share, width), jnp.int16)] * size
                blocks = merge(keep, arrived[g], heads, shapes, True)
                for k, block in zip(groups[g], blocks):
                    parts[k] = across(block, "head", n_head, k) if k else block
            else:
                shapes = [jax.ShapeDtypeStruct((n_head, share, width), jnp.int16)]
                (blocks,) = merge(keep, arrived[g], heads, shapes, True)
                parts = [lax.all_to_all(blocks, "head", split_axis=0, concat_axis=0, tiled=True)]
    return tuple(place(parts, heads, "head", share))


def solution(mesh):
    in_specs = (
        P(("group", "head"), None),
        P(("group", "cache"), None, "head"),
        P(("group", "cache"), None, "head"),
        P(("group", "cache"), None),
        P(("group", "cache")),
    )
    out_specs = (P(("group", "head", "cache"), None), P(("group", "head", "cache"), None))
    return jax.shard_map(
        on_device, mesh=mesh, in_specs=in_specs, out_specs=out_specs, check_vma=False
    )
```

```python
import functools
import math

import jax
import jax.numpy as jnp
from jax import lax
from jax.experimental import pallas as pl
from jax.experimental.pallas import tpu as pltpu
from jax.sharding import PartitionSpec as P

HEADS = 32
DH = 128
PAGE = 128
LANES = 128
TOK_TILE = 256
GROUP = 4
MOST_PERMUTES = 8
VMEM_LIMIT = 50 * 2**20

lowest = -1e30
to_log2 = math.log2(math.e) / math.sqrt(DH)


def attend_kernel(n_parts, starts, limits_ref, *refs):
    q_refs = refs[:n_parts]
    k_hbm, v_hbm, k_first, v_first = refs[n_parts : n_parts + 4]
    out_refs = refs[n_parts + 4 : n_parts + 4 + len(starts)]
    q_turned, k_pool, v_pool, stats, k_sem, v_sem = refs[n_parts + 4 + len(starts) :]
    heads, pool = k_pool.shape[:2]
    all_tok = q_turned.shape[2]
    tile = min(all_tok, TOK_TILE)
    tiles = all_tok // tile
    ahead = min(heads, 3)

    def copies(h):
        columns = pl.ds(pl.multiple_of(h * DH, DH), DH)
        return (
            pltpu.make_async_copy(k_hbm.at[:, :, columns], k_pool.at[h], k_sem.at[h]),
            pltpu.make_async_copy(v_hbm.at[:, :, columns], v_pool.at[h], v_sem.at[h]),
        )

    for h in range(1, ahead):
        for copy in copies(h):
            copy.start()
    k_pool[0] = k_first[...]
    v_pool[0] = v_first[...]
    for h in range(heads):
        rows = [q_ref[:, h * DH : (h + 1) * DH] for q_ref in q_refs[::-1]]
        q_turned[h] = jnp.concatenate(rows, axis=0).T
    stats[...] = jnp.zeros_like(stats)
    ones = jnp.ones((8, PAGE), jnp.bfloat16)

    def unit(u, carry):
        h, t = u // tiles, lax.rem(u, tiles)

        @pl.when(t == 0)
        def _():
            @pl.when(h > 0)
            def _():
                for copy in copies(h):
                    copy.wait()

            @pl.when(h + ahead < heads)
            def _():
                for copy in copies(h + ahead):
                    copy.start()

        start = pl.multiple_of(t * tile, tile)
        columns = pl.ds(start, tile)
        q_tile = q_turned[h, :, columns]
        scores, tops = [], []
        for i in range(0, pool, GROUP):
            block = k_pool[h, i : i + GROUP].reshape(GROUP * PAGE, DH)
            both = jnp.dot(block, q_tile, preferred_element_type=jnp.float32)
            for j in range(GROUP):
                scores.append(both[j * PAGE : (j + 1) * PAGE])
                tops.append(jnp.max(scores[-1], axis=0, keepdims=True))
        used = [jnp.minimum(tops[i], limits_ref[i : i + 1, :]) for i in range(pool)]
        best = functools.reduce(jnp.maximum, used)
        total, accum = 0.0, 0.0
        for i in range(pool):
            weights = jnp.exp2((scores[i] - tops[i]) * to_log2).astype(jnp.bfloat16)
            page_out = jnp.dot(
                jnp.concatenate([v_pool[h, i].T, ones], axis=0),
                weights,
                preferred_element_type=jnp.float32,
            )
            fresh = jnp.exp2((used[i] - best) * to_log2)
            total = total + fresh * page_out[DH : DH + 1]
            accum = accum + fresh * page_out[:DH]
        out = (accum / total).T
        stats[pl.ds(h, 1), columns] = best * to_log2 + jnp.log2(total)
        lanes = pl.ds(pl.multiple_of(h * DH, DH), DH)
        for first, out_ref in zip(starts, out_refs):
            length = out_ref.shape[0]
            if tiles == 1:
                out_ref[:, lanes] = out[first : first + length]
            else:

                @pl.when((start >= first) & (start < first + length))
                def _():
                    out_ref[pl.ds(pl.multiple_of(start - first, tile), tile), lanes] = out

        return carry

    lax.fori_loop(0, heads * tiles, unit, 0)
    for t in range(tiles):
        turned = stats[:, t * tile : (t + 1) * tile].T
        for first, out_ref in zip(starts, out_refs):
            low = max(first, t * tile)
            high = min(first + out_ref.shape[0], (t + 1) * tile)
            if low < high:
                out_ref[low - first : high - first, heads * DH :] = turned[
                    low - t * tile : high - t * tile
                ]


def attend(q_parts, keys, values, limits, starts):
    all_tok = sum(part.shape[0] for part in q_parts)
    pool = keys.shape[0]
    heads = keys.shape[2] // DH
    in_vmem = pl.BlockSpec(memory_space=pltpu.VMEM)
    anywhere = pl.BlockSpec(memory_space=pl.ANY)
    outs = [
        jax.ShapeDtypeStruct((end - first, heads * DH + LANES), jnp.float32)
        for first, end in zip(starts, starts[1:] + [all_tok])
    ]
    return pl.pallas_call(
        functools.partial(attend_kernel, len(q_parts), starts),
        in_specs=[in_vmem] * (1 + len(q_parts)) + [anywhere, anywhere, in_vmem, in_vmem],
        out_specs=[in_vmem] * len(outs),
        scratch_shapes=[
            pltpu.VMEM((heads, DH, all_tok), jnp.bfloat16),
            pltpu.VMEM((heads, pool, PAGE, DH), jnp.bfloat16),
            pltpu.VMEM((heads, pool, PAGE, DH), jnp.bfloat16),
            pltpu.VMEM((LANES, all_tok), jnp.float32),
            pltpu.SemaphoreType.DMA((heads,)),
            pltpu.SemaphoreType.DMA((heads,)),
        ],
        out_shape=outs,
        compiler_params=pltpu.CompilerParams(vmem_limit_bytes=VMEM_LIMIT),
        name="attend",
    )(limits, *q_parts[::-1], keys, values, keys[:, :, :DH], values[:, :, :DH])


def rounded(x):
    return jnp.where(x < 0, x - 0.5, x + 0.5).astype(jnp.int32)


def encode(outs, logs, out_ref):
    heads = len(outs)
    where = (slice(None),) * (len(out_ref.shape) - 1)
    powers = []
    for h, out in enumerate(outs):
        largest = jnp.max(jnp.abs(out), axis=-1, keepdims=True)
        power = jnp.ceil(jnp.log2(jnp.maximum(largest, 2.0**-100)))
        powers.append(power)
        out_ref[where + (slice(h * DH, (h + 1) * DH),)] = rounded(
            out * (jnp.exp2(-power) * 32767.0)
        ).astype(jnp.int16)
    fixed = rounded(logs * 2.0**19)
    high = lax.shift_right_arithmetic(fixed, 16)
    low = lax.bitwise_and(fixed, 65535) - 32768
    pad = jnp.zeros(logs.shape[:-1] + (LANES - 3 * heads,), jnp.int32)
    stat = jnp.concatenate(
        [high[..., :heads], low[..., :heads]] + [p.astype(jnp.int32) for p in powers] + [pad], axis=-1
    )
    out_ref[where + (slice(heads * DH, heads * DH + LANES),)] = stat.astype(jnp.int16)


def decode(heads, ref):
    where = (slice(None),) * (len(ref.shape) - 1)
    stat = ref[where + (slice(heads * DH, heads * DH + LANES),)].astype(jnp.int32)
    fixed = lax.shift_left(stat[..., :heads], 16) + (stat[..., heads : 2 * heads] + 32768)
    logs = fixed.astype(jnp.float32) * 2.0**-19
    steps = jnp.exp2(stat[..., 2 * heads : 3 * heads].astype(jnp.float32)) * (1.0 / 32767.0)
    outs = []
    for h in range(heads):
        coded = ref[where + (slice(h * DH, (h + 1) * DH),)].astype(jnp.int32).astype(jnp.float32)
        outs.append(coded * steps[..., h : h + 1])
    return outs, logs


def plain(heads, ref):
    where = (slice(None),) * (len(ref.shape) - 1)
    outs = [ref[where + (slice(h * DH, (h + 1) * DH),)] for h in range(heads)]
    return outs, ref[where + (slice(heads * DH, heads * DH + heads),)]


def merge_kernel(heads, last, mine_ref, theirs_ref, *out_refs):
    mine, mine_logs = plain(heads, mine_ref)
    theirs, their_logs = (decode if theirs_ref.dtype == jnp.int16 else plain)(heads, theirs_ref)
    top = jnp.maximum(mine_logs, their_logs)
    first, second = jnp.exp2(mine_logs - top), jnp.exp2(their_logs - top)
    both = first + second
    first, second, logs = first / both, second / both, top + jnp.log2(both)
    outs = [
        mine[h] * first[..., h : h + 1] + theirs[h] * second[..., h : h + 1] for h in range(heads)
    ]
    if last:
        if len(out_refs[0].shape) == 3:
            encode(outs, logs, out_refs[0])
        else:
            for block, out_ref in enumerate(out_refs):
                encode([out[block] for out in outs], logs[block], out_ref)
    else:
        keep_ref, send_ref = out_refs
        half = keep_ref.shape[1]
        for h in range(heads):
            keep_ref[:, :, h * DH : (h + 1) * DH] = outs[h][:, :half]
        pad = jnp.zeros(logs.shape[:-1] + (LANES - heads,), jnp.float32)
        keep_ref[:, :, heads * DH :] = jnp.concatenate([logs, pad], axis=-1)[:, :half]
        encode([out[:, half:] for out in outs], logs[:, half:], send_ref)


def merge(mine, theirs, heads, out_shapes, last):
    return pl.pallas_call(
        functools.partial(merge_kernel, heads, last),
        out_shape=out_shapes,
        compiler_params=pltpu.CompilerParams(vmem_limit_bytes=VMEM_LIMIT),
        name="merge",
    )(mine, theirs)


def place_kernel(heads, axis, names, *refs):
    part_refs, (out_ref, logs_ref) = refs[:-2], refs[-2:]
    here = lax.axis_index(axis) if len(part_refs) > 1 else 0
    pieces = []
    if len(part_refs) > 1:
        for k, part_ref in zip(names, part_refs):
            outs, logs = decode(heads, part_ref)
            at = lax.bitwise_xor(here, k)
            out_ref[:, pl.ds(pl.multiple_of(at * heads * DH, DH), heads * DH)] = jnp.concatenate(
                outs, axis=-1
            )
            pieces.append((at, logs))
        columns = []
        for z in range(len(part_refs)):
            columns.append(sum(jnp.where(at == z, logs, 0.0) for at, logs in pieces))
    else:
        outs, logs = decode(heads, part_refs[0])
        for z in range(logs.shape[0]):
            for h in range(heads):
                first = (z * heads + h) * DH
                out_ref[:, first : first + DH] = outs[h][z]
        columns = [logs[z] for z in range(logs.shape[0])]
    logs_ref[...] = jnp.concatenate(columns, axis=-1) * math.log(2.0)


def place(parts, heads, axis, share, names):
    return pl.pallas_call(
        functools.partial(place_kernel, heads, axis, names),
        out_shape=[
            jax.ShapeDtypeStruct((share, HEADS * DH), jnp.float32),
            jax.ShapeDtypeStruct((share, HEADS), jnp.float32),
        ],
        compiler_params=pltpu.CompilerParams(vmem_limit_bytes=VMEM_LIMIT),
        name="place",
    )(*parts)


def across(value, axis, size, bit):
    return lax.ppermute(value, axis, [(i, i ^ bit) for i in range(size)])


def page_limits(page_lists, page_counts, pool, width):
    slots = jnp.arange(page_lists.shape[1], dtype=jnp.int32)
    pages = jnp.arange(pool, dtype=jnp.int32)
    live = jnp.any(
        (page_lists[0][None, :] == pages[:, None]) & (slots < page_counts[0])[None, :], axis=1
    )
    return jnp.broadcast_to(jnp.where(live, -lowest, lowest)[:, None], (pool, width))


def on_device(queries, keys, values, page_lists, page_counts):
    n_head = lax.axis_size("head")
    n_cache = lax.axis_size("cache")
    heads = keys.shape[2] // DH
    share = queries.shape[0] // n_cache
    bits = [1 << i for i in range(n_cache.bit_length() - 1)]
    direct = n_head <= MOST_PERMUTES
    head_at, cache_at = lax.axis_index("head"), lax.axis_index("cache")
    order = [0]
    for bit in reversed(bits):
        order = order + [share_at ^ bit for share_at in order]

    def pick(names, k):
        width = heads * DH
        at = (head_at ^ k) * width
        pieces = [
            lax.dynamic_slice(queries, ((cache_at ^ name) * share, at), (share, width))
            for name in names
        ]
        return jnp.concatenate(pieces)

    half = n_cache // 2
    rows = half * share
    if direct:
        parts = [across(pick(order[:half], k), "head", n_head, k) for k in range(1, n_head)]
        swapped = [across(part, "cache", n_cache, 1) for part in parts]
        q_parts = [pick(order[:half], 0)] + parts + [pick(order[half:], 0)] + swapped
    else:
        shares = queries.reshape(n_cache, share, HEADS * DH)
        same = jnp.concatenate(
            [lax.dynamic_index_in_dim(shares, cache_at ^ name, 0, False) for name in order[:half]]
        )
        moved = lax.all_to_all(
            same.reshape(rows, n_head, heads * DH), "head", split_axis=1, concat_axis=0, tiled=True
        ).reshape(n_head * rows, heads * DH)
        q_parts = [moved, across(moved, "cache", n_cache, 1)]
    all_tok = n_head * queries.shape[0]
    limits = page_limits(page_lists, page_counts, keys.shape[0], min(all_tok, TOK_TILE))
    groups = [range(n_head // 2), range(n_head // 2, n_head)] if direct else [range(n_head)]
    starts = [group[0] * rows for group in groups]
    starts = starts + [n_head * rows + first for first in starts]
    states = attend(q_parts, keys, values, limits, starts)
    width = states[0].shape[1]
    states = [state.reshape(-1, rows, width) for state in states]
    states = list(zip(states[: len(groups)], states[len(groups) :]))[::-1]
    groups = groups[::-1]
    parts = [None] * n_head
    for bit in bits:
        arrived = [across(send, "cache", n_cache, bit) for _, send in states]
        for g, (keep, _) in enumerate(states):
            size, length, _ = keep.shape
            if bit != bits[-1]:
                shapes = [
                    jax.ShapeDtypeStruct((size, length // 2, width), jnp.float32),
                    jax.ShapeDtypeStruct((size, length // 2, width), jnp.int16),
                ]
                states[g] = merge(keep, arrived[g], heads, shapes, False)
            elif direct:
                shapes = [jax.ShapeDtypeStruct((share, width), jnp.int16)] * size
                blocks = merge(keep, arrived[g], heads, shapes, True)
                for k, block in zip(groups[g], blocks):
                    parts[k] = across(block, "head", n_head, k) if k else block
            else:
                shapes = [jax.ShapeDtypeStruct((n_head, share, width), jnp.int16)]
                (blocks,) = merge(keep, arrived[g], heads, shapes, True)
                parts = [lax.all_to_all(blocks, "head", split_axis=0, concat_axis=0, tiled=True)]
    names = list(range(len(parts)))[::-1]
    parts = [parts[k] for k in names]
    return tuple(place(parts, heads, "head", share, names))


def solution(mesh):
    in_specs = (
        P(("group", "head"), None),
        P(("group", "cache"), None, "head"),
        P(("group", "cache"), None, "head"),
        P(("group", "cache"), None),
        P(("group", "cache")),
    )
    out_specs = (P(("group", "head", "cache"), None), P(("group", "head", "cache"), None))
    return jax.shard_map(
        on_device, mesh=mesh, in_specs=in_specs, out_specs=out_specs, check_vma=False
    )
```

```python
import functools
import math

import jax
import jax.numpy as jnp
from jax import lax
from jax.experimental import pallas as pl
from jax.experimental.pallas import tpu as pltpu
from jax.sharding import PartitionSpec as P

HEADS = 32
DH = 128
PAGE = 128
LANES = 128
TOK_TILE = 256
GROUP = 4
MOST_PERMUTES = 8
VMEM_LIMIT = 50 * 2**20

lowest = -1e30
to_log2 = math.log2(math.e) / math.sqrt(DH)


def attend_kernel(n_parts, starts, limits_ref, *refs):
    q_refs = refs[:n_parts]
    k_hbm, v_hbm, k_first, v_first = refs[n_parts : n_parts + 4]
    out_refs = refs[n_parts + 4 : n_parts + 4 + len(starts)]
    q_turned, k_pool, v_pool, stats, k_sem, v_sem = refs[n_parts + 4 + len(starts) :]
    heads, pool = k_pool.shape[:2]
    all_tok = q_turned.shape[2]
    tile = min(all_tok, TOK_TILE)
    tiles = all_tok // tile
    ahead = min(heads, 3)

    def copies(h):
        columns = pl.ds(pl.multiple_of(h * DH, DH), DH)
        return (
            pltpu.make_async_copy(k_hbm.at[:, :, columns], k_pool.at[h], k_sem.at[h]),
            pltpu.make_async_copy(v_hbm.at[:, :, columns], v_pool.at[h], v_sem.at[h]),
        )

    for h in range(1, ahead):
        for copy in copies(h):
            copy.start()
    k_pool[0] = k_first[...]
    v_pool[0] = v_first[...]
    for h in range(heads):
        rows = [q_ref[:, h * DH : (h + 1) * DH] for q_ref in q_refs[::-1]]
        q_turned[h] = jnp.concatenate(rows, axis=0).T
    stats[...] = jnp.zeros_like(stats)
    ones = jnp.ones((8, PAGE), jnp.bfloat16)

    def unit(u, carry):
        h, t = u // tiles, lax.rem(u, tiles)

        @pl.when(t == 0)
        def _():
            @pl.when(h > 0)
            def _():
                for copy in copies(h):
                    copy.wait()

            @pl.when(h + ahead < heads)
            def _():
                for copy in copies(h + ahead):
                    copy.start()

        start = pl.multiple_of(t * tile, tile)
        columns = pl.ds(start, tile)
        q_tile = q_turned[h, :, columns]
        scores, tops = [], []
        for i in range(0, pool, GROUP):
            block = k_pool[h, i : i + GROUP].reshape(GROUP * PAGE, DH)
            both = jnp.dot(block, q_tile, preferred_element_type=jnp.float32)
            for j in range(GROUP):
                scores.append(both[j * PAGE : (j + 1) * PAGE])
                tops.append(jnp.max(scores[-1], axis=0, keepdims=True))
        used = [jnp.minimum(tops[i], limits_ref[i : i + 1, :]) for i in range(pool)]
        best = functools.reduce(jnp.maximum, used)
        total, accum = 0.0, 0.0
        for i in range(pool):
            weights = jnp.exp2((scores[i] - tops[i]) * to_log2).astype(jnp.bfloat16)
            page_out = jnp.dot(
                jnp.concatenate([v_pool[h, i].T, ones], axis=0),
                weights,
                preferred_element_type=jnp.float32,
            )
            fresh = jnp.exp2((used[i] - best) * to_log2)
            total = total + fresh * page_out[DH : DH + 1]
            accum = accum + fresh * page_out[:DH]
        out = (accum / total).T
        stats[pl.ds(h, 1), columns] = best * to_log2 + jnp.log2(total)
        lanes = pl.ds(pl.multiple_of(h * DH, DH), DH)
        for first, out_ref in zip(starts, out_refs):
            length = out_ref.shape[0]
            if tiles == 1:
                out_ref[:, lanes] = out[first : first + length]
            else:

                @pl.when((start >= first) & (start < first + length))
                def _():
                    out_ref[pl.ds(pl.multiple_of(start - first, tile), tile), lanes] = out

        return carry

    lax.fori_loop(0, heads * tiles, unit, 0)
    for t in range(tiles):
        turned = stats[:, t * tile : (t + 1) * tile].T
        for first, out_ref in zip(starts, out_refs):
            low = max(first, t * tile)
            high = min(first + out_ref.shape[0], (t + 1) * tile)
            if low < high:
                out_ref[low - first : high - first, heads * DH :] = turned[
                    low - t * tile : high - t * tile
                ]


def first_kernel(k_hbm, v_hbm, k_ref, v_ref, sems):
    copies = [
        pltpu.make_async_copy(k_hbm.at[:, :, :DH], k_ref, sems.at[0]),
        pltpu.make_async_copy(v_hbm.at[:, :, :DH], v_ref, sems.at[1]),
    ]
    for copy in copies:
        copy.start()
    for copy in copies:
        copy.wait()


def first_head(keys, values):
    out = jax.ShapeDtypeStruct(keys.shape[:2] + (DH,), keys.dtype)
    return pl.pallas_call(
        first_kernel,
        in_specs=[pl.BlockSpec(memory_space=pl.ANY)] * 2,
        out_specs=[pl.BlockSpec(memory_space=pltpu.VMEM)] * 2,
        scratch_shapes=[pltpu.SemaphoreType.DMA((2,))],
        out_shape=[out, out],
        compiler_params=pltpu.CompilerParams(vmem_limit_bytes=VMEM_LIMIT),
        name="first_head",
    )(keys, values)


def attend(q_parts, keys, values, limits, starts):
    all_tok = sum(part.shape[0] for part in q_parts)
    pool = keys.shape[0]
    heads = keys.shape[2] // DH
    in_vmem = pl.BlockSpec(memory_space=pltpu.VMEM)
    anywhere = pl.BlockSpec(memory_space=pl.ANY)
    outs = [
        jax.ShapeDtypeStruct((end - first, heads * DH + LANES), jnp.float32)
        for first, end in zip(starts, starts[1:] + [all_tok])
    ]
    return pl.pallas_call(
        functools.partial(attend_kernel, len(q_parts), starts),
        in_specs=[in_vmem] * (1 + len(q_parts)) + [anywhere, anywhere, in_vmem, in_vmem],
        out_specs=[in_vmem] * len(outs),
        scratch_shapes=[
            pltpu.VMEM((heads, DH, all_tok), jnp.bfloat16),
            pltpu.VMEM((heads, pool, PAGE, DH), jnp.bfloat16),
            pltpu.VMEM((heads, pool, PAGE, DH), jnp.bfloat16),
            pltpu.VMEM((LANES, all_tok), jnp.float32),
            pltpu.SemaphoreType.DMA((heads,)),
            pltpu.SemaphoreType.DMA((heads,)),
        ],
        out_shape=outs,
        compiler_params=pltpu.CompilerParams(vmem_limit_bytes=VMEM_LIMIT),
        name="attend",
    )(limits, *q_parts[::-1], keys, values, *first_head(keys, values))


def rounded(x):
    return jnp.where(x < 0, x - 0.5, x + 0.5).astype(jnp.int32)


def encode(outs, logs, out_ref):
    heads = len(outs)
    where = (slice(None),) * (len(out_ref.shape) - 1)
    powers = []
    for h, out in enumerate(outs):
        largest = jnp.max(jnp.abs(out), axis=-1, keepdims=True)
        power = jnp.ceil(jnp.log2(jnp.maximum(largest, 2.0**-100)))
        powers.append(power)
        out_ref[where + (slice(h * DH, (h + 1) * DH),)] = rounded(
            out * (jnp.exp2(-power) * 32767.0)
        ).astype(jnp.int16)
    fixed = rounded(logs * 2.0**19)
    high = lax.shift_right_arithmetic(fixed, 16)
    low = lax.bitwise_and(fixed, 65535) - 32768
    pad = jnp.zeros(logs.shape[:-1] + (LANES - 3 * heads,), jnp.int32)
    stat = jnp.concatenate(
        [high[..., :heads], low[..., :heads]] + [p.astype(jnp.int32) for p in powers] + [pad], axis=-1
    )
    out_ref[where + (slice(heads * DH, heads * DH + LANES),)] = stat.astype(jnp.int16)


def decode(heads, ref):
    where = (slice(None),) * (len(ref.shape) - 1)
    stat = ref[where + (slice(heads * DH, heads * DH + LANES),)].astype(jnp.int32)
    fixed = lax.shift_left(stat[..., :heads], 16) + (stat[..., heads : 2 * heads] + 32768)
    logs = fixed.astype(jnp.float32) * 2.0**-19
    steps = jnp.exp2(stat[..., 2 * heads : 3 * heads].astype(jnp.float32)) * (1.0 / 32767.0)
    outs = []
    for h in range(heads):
        coded = ref[where + (slice(h * DH, (h + 1) * DH),)].astype(jnp.int32).astype(jnp.float32)
        outs.append(coded * steps[..., h : h + 1])
    return outs, logs


def plain(heads, ref):
    where = (slice(None),) * (len(ref.shape) - 1)
    outs = [ref[where + (slice(h * DH, (h + 1) * DH),)] for h in range(heads)]
    return outs, ref[where + (slice(heads * DH, heads * DH + heads),)]


def merge_kernel(heads, last, mine_ref, theirs_ref, *out_refs):
    mine, mine_logs = plain(heads, mine_ref)
    theirs, their_logs = (decode if theirs_ref.dtype == jnp.int16 else plain)(heads, theirs_ref)
    top = jnp.maximum(mine_logs, their_logs)
    first, second = jnp.exp2(mine_logs - top), jnp.exp2(their_logs - top)
    both = first + second
    first, second, logs = first / both, second / both, top + jnp.log2(both)
    outs = [
        mine[h] * first[..., h : h + 1] + theirs[h] * second[..., h : h + 1] for h in range(heads)
    ]
    if last:
        if len(out_refs[0].shape) == 3:
            encode(outs, logs, out_refs[0])
        else:
            for block, out_ref in enumerate(out_refs):
                encode([out[block] for out in outs], logs[block], out_ref)
    else:
        keep_ref, send_ref = out_refs
        half = keep_ref.shape[1]
        for h in range(heads):
            keep_ref[:, :, h * DH : (h + 1) * DH] = outs[h][:, :half]
        pad = jnp.zeros(logs.shape[:-1] + (LANES - heads,), jnp.float32)
        keep_ref[:, :, heads * DH :] = jnp.concatenate([logs, pad], axis=-1)[:, :half]
        encode([out[:, half:] for out in outs], logs[:, half:], send_ref)


def merge(mine, theirs, heads, out_shapes, last):
    return pl.pallas_call(
        functools.partial(merge_kernel, heads, last),
        out_shape=out_shapes,
        compiler_params=pltpu.CompilerParams(vmem_limit_bytes=VMEM_LIMIT),
        name="merge",
    )(mine, theirs)


def place_kernel(heads, axis, names, *refs):
    part_refs, (out_ref, logs_ref) = refs[:-2], refs[-2:]
    here = lax.axis_index(axis) if len(part_refs) > 1 else 0
    pieces = []
    if len(part_refs) > 1:
        for k, part_ref in zip(names, part_refs):
            outs, logs = decode(heads, part_ref)
            at = lax.bitwise_xor(here, k)
            out_ref[:, pl.ds(pl.multiple_of(at * heads * DH, DH), heads * DH)] = jnp.concatenate(
                outs, axis=-1
            )
            pieces.append((at, logs))
        columns = []
        for z in range(len(part_refs)):
            columns.append(sum(jnp.where(at == z, logs, 0.0) for at, logs in pieces))
    else:
        outs, logs = decode(heads, part_refs[0])
        for z in range(logs.shape[0]):
            for h in range(heads):
                first = (z * heads + h) * DH
                out_ref[:, first : first + DH] = outs[h][z]
        columns = [logs[z] for z in range(logs.shape[0])]
    logs_ref[...] = jnp.concatenate(columns, axis=-1) * math.log(2.0)


def place(parts, heads, axis, share, names):
    return pl.pallas_call(
        functools.partial(place_kernel, heads, axis, names),
        out_shape=[
            jax.ShapeDtypeStruct((share, HEADS * DH), jnp.float32),
            jax.ShapeDtypeStruct((share, HEADS), jnp.float32),
        ],
        compiler_params=pltpu.CompilerParams(vmem_limit_bytes=VMEM_LIMIT),
        name="place",
    )(*parts)


def across(value, axis, size, bit):
    return lax.ppermute(value, axis, [(i, i ^ bit) for i in range(size)])


def page_limits(page_lists, page_counts, pool, width):
    slots = jnp.arange(page_lists.shape[1], dtype=jnp.int32)
    pages = jnp.arange(pool, dtype=jnp.int32)
    live = jnp.any(
        (page_lists[0][None, :] == pages[:, None]) & (slots < page_counts[0])[None, :], axis=1
    )
    return jnp.broadcast_to(jnp.where(live, -lowest, lowest)[:, None], (pool, width))


def on_device(queries, keys, values, page_lists, page_counts):
    n_head = lax.axis_size("head")
    n_cache = lax.axis_size("cache")
    heads = keys.shape[2] // DH
    share = queries.shape[0] // n_cache
    bits = [1 << i for i in range(n_cache.bit_length() - 1)]
    direct = n_head <= MOST_PERMUTES
    head_at, cache_at = lax.axis_index("head"), lax.axis_index("cache")
    order = [0]
    for bit in reversed(bits):
        order = order + [share_at ^ bit for share_at in order]

    def pick(names, k):
        width = heads * DH
        at = (head_at ^ k) * width
        pieces = [
            lax.dynamic_slice(queries, ((cache_at ^ name) * share, at), (share, width))
            for name in names
        ]
        return jnp.concatenate(pieces)

    half = n_cache // 2
    rows = half * share
    if direct:
        parts = [across(pick(order[:half], k), "head", n_head, k) for k in range(1, n_head)]
        swapped = [across(part, "cache", n_cache, 1) for part in parts]
        q_parts = [pick(order[:half], 0)] + parts + [pick(order[half:], 0)] + swapped
    else:
        shares = queries.reshape(n_cache, share, HEADS * DH)
        same = jnp.concatenate(
            [lax.dynamic_index_in_dim(shares, cache_at ^ name, 0, False) for name in order[:half]]
        )
        moved = lax.all_to_all(
            same.reshape(rows, n_head, heads * DH), "head", split_axis=1, concat_axis=0, tiled=True
        ).reshape(n_head * rows, heads * DH)
        q_parts = [moved, across(moved, "cache", n_cache, 1)]
    all_tok = n_head * queries.shape[0]
    limits = page_limits(page_lists, page_counts, keys.shape[0], min(all_tok, TOK_TILE))
    groups = [range(n_head // 2), range(n_head // 2, n_head)] if direct else [range(n_head)]
    starts = [group[0] * rows for group in groups]
    starts = starts + [n_head * rows + first for first in starts]
    states = attend(q_parts, keys, values, limits, starts)
    width = states[0].shape[1]
    states = [state.reshape(-1, rows, width) for state in states]
    states = list(zip(states[: len(groups)], states[len(groups) :]))[::-1]
    groups = groups[::-1]
    parts = [None] * n_head
    for bit in bits:
        arrived = [across(send, "cache", n_cache, bit) for _, send in states]
        for g, (keep, _) in enumerate(states):
            size, length, _ = keep.shape
            if bit != bits[-1]:
                shapes = [
                    jax.ShapeDtypeStruct((size, length // 2, width), jnp.float32),
                    jax.ShapeDtypeStruct((size, length // 2, width), jnp.int16),
                ]
                states[g] = merge(keep, arrived[g], heads, shapes, False)
            elif direct:
                shapes = [jax.ShapeDtypeStruct((share, width), jnp.int16)] * size
                blocks = merge(keep, arrived[g], heads, shapes, True)
                for k, block in zip(groups[g], blocks):
                    parts[k] = across(block, "head", n_head, k) if k else block
            else:
                shapes = [jax.ShapeDtypeStruct((n_head, share, width), jnp.int16)]
                (blocks,) = merge(keep, arrived[g], heads, shapes, True)
                parts = [lax.all_to_all(blocks, "head", split_axis=0, concat_axis=0, tiled=True)]
    names = list(range(len(parts)))[::-1]
    parts = [parts[k] for k in names]
    return tuple(place(parts, heads, "head", share, names))


def solution(mesh):
    in_specs = (
        P(("group", "head"), None),
        P(("group", "cache"), None, "head"),
        P(("group", "cache"), None, "head"),
        P(("group", "cache"), None),
        P(("group", "cache")),
    )
    out_specs = (P(("group", "head", "cache"), None), P(("group", "head", "cache"), None))
    return jax.shard_map(
        on_device, mesh=mesh, in_specs=in_specs, out_specs=out_specs, check_vma=False
    )
```

```python
import functools
import math

import jax
import jax.numpy as jnp
from jax import lax
from jax.experimental import pallas as pl
from jax.experimental.pallas import tpu as pltpu
from jax.sharding import PartitionSpec as P

HEADS = 32
DH = 128
PAGE = 128
LANES = 128
TOK_TILE = 256
GROUP = 4
MOST_PERMUTES = 8
VMEM_LIMIT = 50 * 2**20

lowest = -1e30
to_log2 = math.log2(math.e) / math.sqrt(DH)


def attend_kernel(n_parts, starts, limits_ref, *refs):
    q_refs = refs[:n_parts]
    k_hbm, v_hbm, k_first, v_first = refs[n_parts : n_parts + 4]
    out_refs = refs[n_parts + 4 : n_parts + 4 + len(starts)]
    q_turned, k_pool, v_pool, stats, k_sem, v_sem = refs[n_parts + 4 + len(starts) :]
    heads, pool = k_pool.shape[:2]
    all_tok = q_turned.shape[2]
    tile = min(all_tok, TOK_TILE)
    tiles = all_tok // tile
    ahead = min(heads, 3)

    def copies(h):
        columns = pl.ds(pl.multiple_of(h * DH, DH), DH)
        return (
            pltpu.make_async_copy(k_hbm.at[:, :, columns], k_pool.at[h], k_sem.at[h]),
            pltpu.make_async_copy(v_hbm.at[:, :, columns], v_pool.at[h], v_sem.at[h]),
        )

    for h in range(1, ahead):
        for copy in copies(h):
            copy.start()
    k_pool[0] = k_first[...]
    v_pool[0] = v_first[...]
    def turn(h):
        lanes = pl.ds(pl.multiple_of(h * DH, DH), DH)
        q_turned[h] = jnp.concatenate([q_ref[:, lanes] for q_ref in q_refs[::-1]], axis=0).T

    for h in range(1 if tiles == 1 else heads):
        turn(h)
    stats[...] = jnp.zeros_like(stats)
    ones = jnp.ones((8, PAGE), jnp.bfloat16)

    def unit(u, carry):
        h, t = u // tiles, lax.rem(u, tiles)

        @pl.when(t == 0)
        def _():
            @pl.when(h > 0)
            def _():
                for copy in copies(h):
                    copy.wait()

            @pl.when(h + ahead < heads)
            def _():
                for copy in copies(h + ahead):
                    copy.start()

        start = pl.multiple_of(t * tile, tile)
        columns = pl.ds(start, tile)
        q_tile = q_turned[h, :, columns]
        if tiles == 1:
            turn(jnp.minimum(h + 1, heads - 1))
        scores, tops = [], []
        for i in range(0, pool, GROUP):
            block = k_pool[h, i : i + GROUP].reshape(GROUP * PAGE, DH)
            both = jnp.dot(block, q_tile, preferred_element_type=jnp.float32)
            for j in range(GROUP):
                scores.append(both[j * PAGE : (j + 1) * PAGE])
                tops.append(jnp.max(scores[-1], axis=0, keepdims=True))
        used = [jnp.minimum(tops[i], limits_ref[i : i + 1, :]) for i in range(pool)]
        best = functools.reduce(jnp.maximum, used)
        total, accum = 0.0, 0.0
        for i in range(pool):
            weights = jnp.exp2((scores[i] - tops[i]) * to_log2).astype(jnp.bfloat16)
            page_out = jnp.dot(
                jnp.concatenate([v_pool[h, i].T, ones], axis=0),
                weights,
                preferred_element_type=jnp.float32,
            )
            fresh = jnp.exp2((used[i] - best) * to_log2)
            total = total + fresh * page_out[DH : DH + 1]
            accum = accum + fresh * page_out[:DH]
        out = accum / total
        stats[pl.ds(h, 1), columns] = best * to_log2 + jnp.log2(total)
        stats[pl.ds(heads + h, 1), columns] = jnp.max(jnp.abs(out), axis=0, keepdims=True)
        out = out.T
        lanes = pl.ds(pl.multiple_of(h * DH, DH), DH)
        for first, out_ref in zip(starts, out_refs):
            length = out_ref.shape[0]
            if tiles == 1:
                out_ref[:, lanes] = out[first : first + length]
            else:

                @pl.when((start >= first) & (start < first + length))
                def _():
                    out_ref[pl.ds(pl.multiple_of(start - first, tile), tile), lanes] = out

        return carry

    lax.fori_loop(0, heads * tiles, unit, 0)
    for t in range(tiles):
        turned = stats[:, t * tile : (t + 1) * tile].T
        for first, out_ref in zip(starts, out_refs):
            low = max(first, t * tile)
            high = min(first + out_ref.shape[0], (t + 1) * tile)
            if low < high:
                out_ref[low - first : high - first, heads * DH :] = turned[
                    low - t * tile : high - t * tile
                ]


def first_kernel(k_hbm, v_hbm, k_ref, v_ref, sems):
    copies = [
        pltpu.make_async_copy(k_hbm.at[:, :, :DH], k_ref, sems.at[0]),
        pltpu.make_async_copy(v_hbm.at[:, :, :DH], v_ref, sems.at[1]),
    ]
    for copy in copies:
        copy.start()
    for copy in copies:
        copy.wait()


def first_head(keys, values):
    out = jax.ShapeDtypeStruct(keys.shape[:2] + (DH,), keys.dtype)
    return pl.pallas_call(
        first_kernel,
        in_specs=[pl.BlockSpec(memory_space=pl.ANY)] * 2,
        out_specs=[pl.BlockSpec(memory_space=pltpu.VMEM)] * 2,
        scratch_shapes=[pltpu.SemaphoreType.DMA((2,))],
        out_shape=[out, out],
        compiler_params=pltpu.CompilerParams(vmem_limit_bytes=VMEM_LIMIT),
        name="first_head",
    )(keys, values)


def attend(q_parts, keys, values, limits, starts):
    all_tok = sum(part.shape[0] for part in q_parts)
    pool = keys.shape[0]
    heads = keys.shape[2] // DH
    in_vmem = pl.BlockSpec(memory_space=pltpu.VMEM)
    anywhere = pl.BlockSpec(memory_space=pl.ANY)
    outs = [
        jax.ShapeDtypeStruct((end - first, heads * DH + LANES), jnp.float32)
        for first, end in zip(starts, starts[1:] + [all_tok])
    ]
    return pl.pallas_call(
        functools.partial(attend_kernel, len(q_parts), starts),
        in_specs=[in_vmem] * (1 + len(q_parts)) + [anywhere, anywhere, in_vmem, in_vmem],
        out_specs=[in_vmem] * len(outs),
        scratch_shapes=[
            pltpu.VMEM((heads, DH, all_tok), jnp.bfloat16),
            pltpu.VMEM((heads, pool, PAGE, DH), jnp.bfloat16),
            pltpu.VMEM((heads, pool, PAGE, DH), jnp.bfloat16),
            pltpu.VMEM((LANES, all_tok), jnp.float32),
            pltpu.SemaphoreType.DMA((heads,)),
            pltpu.SemaphoreType.DMA((heads,)),
        ],
        out_shape=outs,
        compiler_params=pltpu.CompilerParams(vmem_limit_bytes=VMEM_LIMIT),
        name="attend",
    )(limits, *q_parts[::-1], keys, values, *first_head(keys, values))


def rounded(x):
    return jnp.where(x < 0, x - 0.5, x + 0.5).astype(jnp.int32)


def write_stats(logs, powers, out_ref, heads):
    fixed = rounded(logs * 2.0**19)
    high = lax.shift_right_arithmetic(fixed, 16)
    low = lax.bitwise_and(fixed, 65535) - 32768
    pad = jnp.zeros(logs.shape[:-1] + (LANES - 3 * heads,), jnp.int32)
    stat = jnp.concatenate([high, low, powers.astype(jnp.int32), pad], axis=-1)
    where = (slice(None),) * (len(out_ref.shape) - 1)
    out_ref[where + (slice(heads * DH, heads * DH + LANES),)] = stat.astype(jnp.int16)


def decode(heads, ref):
    where = (slice(None),) * (len(ref.shape) - 1)
    stat = ref[where + (slice(heads * DH, heads * DH + LANES),)].astype(jnp.int32)
    fixed = lax.shift_left(stat[..., :heads], 16) + (stat[..., heads : 2 * heads] + 32768)
    logs = fixed.astype(jnp.float32) * 2.0**-19
    steps = jnp.exp2(stat[..., 2 * heads : 3 * heads].astype(jnp.float32)) * (1.0 / 32767.0)
    outs = []
    for h in range(heads):
        coded = ref[where + (slice(h * DH, (h + 1) * DH),)].astype(jnp.int32).astype(jnp.float32)
        outs.append(coded * steps[..., h : h + 1])
    return outs, logs


def merge_kernel(heads, last, mine_ref, theirs_ref, *out_refs):
    def lanes(h):
        return slice(h * DH, (h + 1) * DH)

    first_stat = heads * DH
    mine_logs = mine_ref[:, :, first_stat : first_stat + heads]
    mine_bound = mine_ref[:, :, first_stat + heads : first_stat + 2 * heads]
    coded = theirs_ref.dtype == jnp.int16
    if coded:
        stat = theirs_ref[:, :, first_stat:].astype(jnp.int32)
        fixed = lax.shift_left(stat[..., :heads], 16) + (stat[..., heads : 2 * heads] + 32768)
        their_logs = fixed.astype(jnp.float32) * 2.0**-19
        their_bound = jnp.exp2(stat[..., 2 * heads : 3 * heads].astype(jnp.float32))
    else:
        their_logs = theirs_ref[:, :, first_stat : first_stat + heads]
        their_bound = theirs_ref[:, :, first_stat + heads : first_stat + 2 * heads]
    top = jnp.maximum(mine_logs, their_logs)
    first, second = jnp.exp2(mine_logs - top), jnp.exp2(their_logs - top)
    both = first + second
    first, second, logs = first / both, second / both, top + jnp.log2(both)
    bound = first * mine_bound + second * their_bound
    powers = jnp.ceil(jnp.log2(jnp.maximum(bound, 2.0**-100)) + 0.001)
    scale = jnp.exp2(-powers) * 32767.0
    if coded:
        second = second * their_bound * (1.0 / 32767.0)
    first_coded, second_coded = first * scale, second * scale

    def joined(h, a, b, rows):
        theirs = theirs_ref[:, rows, lanes(h)]
        if coded:
            theirs = theirs.astype(jnp.int32).astype(jnp.float32)
        return mine_ref[:, rows, lanes(h)] * a[:, rows, h : h + 1] + theirs * b[:, rows, h : h + 1]

    if last:
        everything = slice(0, mine_ref.shape[1])
        for h in range(heads):
            out = rounded(joined(h, first_coded, second_coded, everything)).astype(jnp.int16)
            if len(out_refs[0].shape) == 3:
                out_refs[0][:, :, lanes(h)] = out
            else:
                for block, out_ref in enumerate(out_refs):
                    out_ref[:, lanes(h)] = out[block]
        if len(out_refs[0].shape) == 3:
            write_stats(logs, powers, out_refs[0], heads)
        else:
            for block, out_ref in enumerate(out_refs):
                write_stats(logs[block], powers[block], out_ref, heads)
    else:
        keep_ref, send_ref = out_refs
        half = keep_ref.shape[1]
        low, high = slice(0, half), slice(half, 2 * half)
        for h in range(heads):
            keep_ref[:, :, lanes(h)] = joined(h, first, second, low)
            out = rounded(joined(h, first_coded, second_coded, high))
            send_ref[:, :, lanes(h)] = out.astype(jnp.int16)
        pad = jnp.zeros(logs.shape[:-1] + (LANES - 2 * heads,), jnp.float32)
        keep_ref[:, :, first_stat:] = jnp.concatenate([logs, bound, pad], axis=-1)[:, low]
        write_stats(logs[:, high], powers[:, high], send_ref, heads)


def merge(mine, theirs, heads, out_shapes, last):
    return pl.pallas_call(
        functools.partial(merge_kernel, heads, last),
        out_shape=out_shapes,
        compiler_params=pltpu.CompilerParams(vmem_limit_bytes=VMEM_LIMIT),
        name="merge",
    )(mine, theirs)


def place_kernel(heads, axis, names, *refs):
    part_refs, (out_ref, logs_ref) = refs[:-2], refs[-2:]
    here = lax.axis_index(axis) if len(part_refs) > 1 else 0
    pieces = []
    if len(part_refs) > 1:
        for k, part_ref in zip(names, part_refs):
            outs, logs = decode(heads, part_ref)
            at = lax.bitwise_xor(here, k)
            out_ref[:, pl.ds(pl.multiple_of(at * heads * DH, DH), heads * DH)] = jnp.concatenate(
                outs, axis=-1
            )
            pieces.append((at, logs))
        columns = []
        for z in range(len(part_refs)):
            columns.append(sum(jnp.where(at == z, logs, 0.0) for at, logs in pieces))
    else:
        outs, logs = decode(heads, part_refs[0])
        for z in range(logs.shape[0]):
            for h in range(heads):
                first = (z * heads + h) * DH
                out_ref[:, first : first + DH] = outs[h][z]
        columns = [logs[z] for z in range(logs.shape[0])]
    logs_ref[...] = jnp.concatenate(columns, axis=-1) * math.log(2.0)


def place(parts, heads, axis, share, names):
    return pl.pallas_call(
        functools.partial(place_kernel, heads, axis, names),
        out_shape=[
            jax.ShapeDtypeStruct((share, HEADS * DH), jnp.float32),
            jax.ShapeDtypeStruct((share, HEADS), jnp.float32),
        ],
        compiler_params=pltpu.CompilerParams(vmem_limit_bytes=VMEM_LIMIT),
        name="place",
    )(*parts)


def across(value, axis, size, bit):
    return lax.ppermute(value, axis, [(i, i ^ bit) for i in range(size)])


def page_limits(page_lists, page_counts, pool, width):
    slots = jnp.arange(page_lists.shape[1], dtype=jnp.int32)
    pages = jnp.arange(pool, dtype=jnp.int32)
    live = jnp.any(
        (page_lists[0][None, :] == pages[:, None]) & (slots < page_counts[0])[None, :], axis=1
    )
    return jnp.broadcast_to(jnp.where(live, -lowest, lowest)[:, None], (pool, width))


def on_device(queries, keys, values, page_lists, page_counts):
    n_head = lax.axis_size("head")
    n_cache = lax.axis_size("cache")
    heads = keys.shape[2] // DH
    share = queries.shape[0] // n_cache
    bits = [1 << i for i in range(n_cache.bit_length() - 1)]
    direct = n_head <= MOST_PERMUTES
    head_at, cache_at = lax.axis_index("head"), lax.axis_index("cache")
    order = [0]
    for bit in reversed(bits):
        order = order + [share_at ^ bit for share_at in order]

    def pick(names, k):
        width = heads * DH
        at = (head_at ^ k) * width
        pieces = [
            lax.dynamic_slice(queries, ((cache_at ^ name) * share, at), (share, width))
            for name in names
        ]
        return jnp.concatenate(pieces)

    half = n_cache // 2
    rows = half * share
    if direct:
        parts = [across(pick(order[:half], k), "head", n_head, k) for k in range(1, n_head)]
        swapped = [across(part, "cache", n_cache, 1) for part in parts]
        q_parts = [pick(order[:half], 0)] + parts + [pick(order[half:], 0)] + swapped
    else:
        shares = queries.reshape(n_cache, share, HEADS * DH)
        same = jnp.concatenate(
            [lax.dynamic_index_in_dim(shares, cache_at ^ name, 0, False) for name in order[:half]]
        )
        moved = lax.all_to_all(
            same.reshape(rows, n_head, heads * DH), "head", split_axis=1, concat_axis=0, tiled=True
        ).reshape(n_head * rows, heads * DH)
        q_parts = [moved, across(moved, "cache", n_cache, 1)]
    all_tok = n_head * queries.shape[0]
    limits = page_limits(page_lists, page_counts, keys.shape[0], min(all_tok, TOK_TILE))
    groups = [range(n_head // 2), range(n_head // 2, n_head)] if direct else [range(n_head)]
    starts = [group[0] * rows for group in groups]
    starts = starts + [n_head * rows + first for first in starts]
    states = attend(q_parts, keys, values, limits, starts)
    width = states[0].shape[1]
    states = [state.reshape(-1, rows, width) for state in states]
    states = list(zip(states[: len(groups)], states[len(groups) :]))[::-1]
    groups = groups[::-1]
    parts = [None] * n_head
    for bit in bits:
        arrived = [across(send, "cache", n_cache, bit) for _, send in states]
        for g, (keep, _) in enumerate(states):
            size, length, _ = keep.shape
            if bit != bits[-1]:
                shapes = [
                    jax.ShapeDtypeStruct((size, length // 2, width), jnp.float32),
                    jax.ShapeDtypeStruct((size, length // 2, width), jnp.int16),
                ]
                states[g] = merge(keep, arrived[g], heads, shapes, False)
            elif direct:
                shapes = [jax.ShapeDtypeStruct((share, width), jnp.int16)] * size
                blocks = merge(keep, arrived[g], heads, shapes, True)
                for k, block in zip(groups[g], blocks):
                    parts[k] = across(block, "head", n_head, k) if k else block
            else:
                shapes = [jax.ShapeDtypeStruct((n_head, share, width), jnp.int16)]
                (blocks,) = merge(keep, arrived[g], heads, shapes, True)
                parts = [lax.all_to_all(blocks, "head", split_axis=0, concat_axis=0, tiled=True)]
    names = list(range(len(parts)))[::-1]
    parts = [parts[k] for k in names]
    return tuple(place(parts, heads, "head", share, names))


def solution(mesh):
    in_specs = (
        P(("group", "head"), None),
        P(("group", "cache"), None, "head"),
        P(("group", "cache"), None, "head"),
        P(("group", "cache"), None),
        P(("group", "cache")),
    )
    out_specs = (P(("group", "head", "cache"), None), P(("group", "head", "cache"), None))
    return jax.shard_map(
        on_device, mesh=mesh, in_specs=in_specs, out_specs=out_specs, check_vma=False
    )
```

```python
import functools
import math

import jax
import jax.numpy as jnp
from jax import lax
from jax.experimental import pallas as pl
from jax.experimental.pallas import tpu as pltpu
from jax.sharding import PartitionSpec as P

HEADS = 32
DH = 128
PAGE = 128
LANES = 128
TOK_TILE = 256
GROUP = 4
MOST_PERMUTES = 8
VMEM_LIMIT = 50 * 2**20

lowest = -1e30
to_log2 = math.log2(math.e) / math.sqrt(DH)


def attend_kernel(n_parts, starts, limits_ref, *refs):
    q_refs = refs[:n_parts]
    k_hbm, v_hbm, k_first, v_first = refs[n_parts : n_parts + 4]
    out_refs = refs[n_parts + 4 : n_parts + 4 + len(starts)]
    q_turned, k_pool, v_pool, stats, k_sem, v_sem = refs[n_parts + 4 + len(starts) :]
    heads, pool = k_pool.shape[:2]
    all_tok = q_turned.shape[2]
    tile = min(all_tok, TOK_TILE)
    tiles = all_tok // tile
    ahead = min(heads, 3)

    def copies(h):
        columns = pl.ds(pl.multiple_of(h * DH, DH), DH)
        return (
            pltpu.make_async_copy(k_hbm.at[:, :, columns], k_pool.at[h], k_sem.at[h]),
            pltpu.make_async_copy(v_hbm.at[:, :, columns], v_pool.at[h], v_sem.at[h]),
        )

    for h in range(1, ahead):
        for copy in copies(h):
            copy.start()
    k_pool[0] = k_first[...]
    v_pool[0] = v_first[...]
    def turn(h):
        lanes = pl.ds(pl.multiple_of(h * DH, DH), DH)
        q_turned[h] = jnp.concatenate([q_ref[:, lanes] for q_ref in q_refs[::-1]], axis=0).T

    for h in range(1 if tiles == 1 else heads):
        turn(h)
    stats[...] = jnp.zeros_like(stats)
    ones = jnp.ones((8, PAGE), jnp.bfloat16)

    def unit(u, carry):
        h, t = u // tiles, lax.rem(u, tiles)

        @pl.when(t == 0)
        def _():
            @pl.when(h > 0)
            def _():
                for copy in copies(h):
                    copy.wait()

            @pl.when(h + ahead < heads)
            def _():
                for copy in copies(h + ahead):
                    copy.start()

        start = pl.multiple_of(t * tile, tile)
        columns = pl.ds(start, tile)
        q_tile = q_turned[h, :, columns]
        if tiles == 1:
            turn(jnp.minimum(h + 1, heads - 1))
        scores, tops = [], []
        for i in range(0, pool, GROUP):
            block = k_pool[h, i : i + GROUP].reshape(GROUP * PAGE, DH)
            both = jnp.dot(block, q_tile, preferred_element_type=jnp.float32)
            for j in range(GROUP):
                scores.append(both[j * PAGE : (j + 1) * PAGE])
                tops.append(jnp.max(scores[-1], axis=0, keepdims=True))
        used = [jnp.minimum(tops[i], limits_ref[i : i + 1, :]) for i in range(pool)]
        best = functools.reduce(jnp.maximum, used)
        total, accum = 0.0, 0.0
        for i in range(pool):
            weights = jnp.exp2((scores[i] - tops[i]) * to_log2).astype(jnp.bfloat16)
            page_out = jnp.dot(
                jnp.concatenate([v_pool[h, i].T, ones], axis=0),
                weights,
                preferred_element_type=jnp.float32,
            )
            fresh = jnp.exp2((used[i] - best) * to_log2)
            total = total + fresh * page_out[DH : DH + 1]
            accum = accum + fresh * page_out[:DH]
        out = accum * (1.0 / total)
        stats[pl.ds(h, 1), columns] = best * to_log2 + jnp.log2(total)
        stats[pl.ds(heads + h, 1), columns] = jnp.max(jnp.abs(out), axis=0, keepdims=True)
        out = out.T
        lanes = pl.ds(pl.multiple_of(h * DH, DH), DH)
        for first, out_ref in zip(starts, out_refs):
            length = out_ref.shape[0]
            if tiles == 1:
                out_ref[:, lanes] = out[first : first + length]
            else:

                @pl.when((start >= first) & (start < first + length))
                def _():
                    out_ref[pl.ds(pl.multiple_of(start - first, tile), tile), lanes] = out

        return carry

    lax.fori_loop(0, heads * tiles, unit, 0)
    for t in range(tiles):
        turned = stats[:, t * tile : (t + 1) * tile].T
        for first, out_ref in zip(starts, out_refs):
            low = max(first, t * tile)
            high = min(first + out_ref.shape[0], (t + 1) * tile)
            if low < high:
                out_ref[low - first : high - first, heads * DH :] = turned[
                    low - t * tile : high - t * tile
                ]


def first_kernel(k_hbm, v_hbm, k_ref, v_ref, sems):
    copies = [
        pltpu.make_async_copy(k_hbm.at[:, :, :DH], k_ref, sems.at[0]),
        pltpu.make_async_copy(v_hbm.at[:, :, :DH], v_ref, sems.at[1]),
    ]
    for copy in copies:
        copy.start()
    for copy in copies:
        copy.wait()


def first_head(keys, values):
    out = jax.ShapeDtypeStruct(keys.shape[:2] + (DH,), keys.dtype)
    return pl.pallas_call(
        first_kernel,
        in_specs=[pl.BlockSpec(memory_space=pl.ANY)] * 2,
        out_specs=[pl.BlockSpec(memory_space=pltpu.VMEM)] * 2,
        scratch_shapes=[pltpu.SemaphoreType.DMA((2,))],
        out_shape=[out, out],
        compiler_params=pltpu.CompilerParams(vmem_limit_bytes=VMEM_LIMIT),
        name="first_head",
    )(keys, values)


def attend(q_parts, keys, values, limits, starts):
    all_tok = sum(part.shape[0] for part in q_parts)
    pool = keys.shape[0]
    heads = keys.shape[2] // DH
    in_vmem = pl.BlockSpec(memory_space=pltpu.VMEM)
    anywhere = pl.BlockSpec(memory_space=pl.ANY)
    outs = [
        jax.ShapeDtypeStruct((end - first, heads * DH + LANES), jnp.float32)
        for first, end in zip(starts, starts[1:] + [all_tok])
    ]
    return pl.pallas_call(
        functools.partial(attend_kernel, len(q_parts), starts),
        in_specs=[in_vmem] * (1 + len(q_parts)) + [anywhere, anywhere, in_vmem, in_vmem],
        out_specs=[in_vmem] * len(outs),
        scratch_shapes=[
            pltpu.VMEM((heads, DH, all_tok), jnp.bfloat16),
            pltpu.VMEM((heads, pool, PAGE, DH), jnp.bfloat16),
            pltpu.VMEM((heads, pool, PAGE, DH), jnp.bfloat16),
            pltpu.VMEM((LANES, all_tok), jnp.float32),
            pltpu.SemaphoreType.DMA((heads,)),
            pltpu.SemaphoreType.DMA((heads,)),
        ],
        out_shape=outs,
        compiler_params=pltpu.CompilerParams(vmem_limit_bytes=VMEM_LIMIT),
        name="attend",
    )(limits, *q_parts[::-1], keys, values, *first_head(keys, values))


def rounded(x):
    return jnp.where(x < 0, x - 0.5, x + 0.5).astype(jnp.int32)


def write_stats(logs, powers, out_ref, heads):
    fixed = rounded(logs * 2.0**19)
    high = lax.shift_right_arithmetic(fixed, 16)
    low = lax.bitwise_and(fixed, 65535) - 32768
    pad = jnp.zeros(logs.shape[:-1] + (LANES - 3 * heads,), jnp.int32)
    stat = jnp.concatenate([high, low, powers.astype(jnp.int32), pad], axis=-1)
    where = (slice(None),) * (len(out_ref.shape) - 1)
    out_ref[where + (slice(heads * DH, heads * DH + LANES),)] = stat.astype(jnp.int16)


def decode(heads, ref):
    where = (slice(None),) * (len(ref.shape) - 1)
    stat = ref[where + (slice(heads * DH, heads * DH + LANES),)].astype(jnp.int32)
    fixed = lax.shift_left(stat[..., :heads], 16) + (stat[..., heads : 2 * heads] + 32768)
    logs = fixed.astype(jnp.float32) * 2.0**-19
    steps = jnp.exp2(stat[..., 2 * heads : 3 * heads].astype(jnp.float32)) * (1.0 / 32767.0)
    outs = []
    for h in range(heads):
        coded = ref[where + (slice(h * DH, (h + 1) * DH),)].astype(jnp.int32).astype(jnp.float32)
        outs.append(coded * steps[..., h : h + 1])
    return outs, logs


def merge_kernel(heads, last, mine_ref, theirs_ref, *out_refs):
    def lanes(h):
        return slice(h * DH, (h + 1) * DH)

    first_stat = heads * DH
    mine_logs = mine_ref[:, :, first_stat : first_stat + heads]
    mine_bound = mine_ref[:, :, first_stat + heads : first_stat + 2 * heads]
    coded = theirs_ref.dtype == jnp.int16
    if coded:
        stat = theirs_ref[:, :, first_stat:].astype(jnp.int32)
        fixed = lax.shift_left(stat[..., :heads], 16) + (stat[..., heads : 2 * heads] + 32768)
        their_logs = fixed.astype(jnp.float32) * 2.0**-19
        their_bound = jnp.exp2(stat[..., 2 * heads : 3 * heads].astype(jnp.float32))
    else:
        their_logs = theirs_ref[:, :, first_stat : first_stat + heads]
        their_bound = theirs_ref[:, :, first_stat + heads : first_stat + 2 * heads]
    top = jnp.maximum(mine_logs, their_logs)
    first, second = jnp.exp2(mine_logs - top), jnp.exp2(their_logs - top)
    both = first + second
    first, second, logs = first / both, second / both, top + jnp.log2(both)
    bound = first * mine_bound + second * their_bound
    powers = jnp.ceil(jnp.log2(jnp.maximum(bound, 2.0**-100)) + 0.001)
    scale = jnp.exp2(-powers) * 32767.0
    if coded:
        second = second * their_bound * (1.0 / 32767.0)
    first_coded, second_coded = first * scale, second * scale

    def joined(h, a, b, rows):
        if coded:
            theirs = theirs_ref[:, :, lanes(h)].astype(jnp.int32).astype(jnp.float32)[:, rows]
        else:
            theirs = theirs_ref[:, rows, lanes(h)]
        return mine_ref[:, rows, lanes(h)] * a[:, rows, h : h + 1] + theirs * b[:, rows, h : h + 1]

    if last:
        everything = slice(0, mine_ref.shape[1])
        for h in range(heads):
            out = rounded(joined(h, first_coded, second_coded, everything)).astype(jnp.int16)
            if len(out_refs[0].shape) == 3:
                out_refs[0][:, :, lanes(h)] = out
            else:
                for block, out_ref in enumerate(out_refs):
                    out_ref[:, lanes(h)] = out[block]
        if len(out_refs[0].shape) == 3:
            write_stats(logs, powers, out_refs[0], heads)
        else:
            for block, out_ref in enumerate(out_refs):
                write_stats(logs[block], powers[block], out_ref, heads)
    else:
        keep_ref, send_ref = out_refs
        half = keep_ref.shape[1]
        low, high = slice(0, half), slice(half, 2 * half)
        for h in range(heads):
            keep_ref[:, :, lanes(h)] = joined(h, first, second, low)
            out = rounded(joined(h, first_coded, second_coded, high))
            send_ref[:, :, lanes(h)] = out.astype(jnp.int16)
        pad = jnp.zeros(logs.shape[:-1] + (LANES - 2 * heads,), jnp.float32)
        keep_ref[:, :, first_stat:] = jnp.concatenate([logs, bound, pad], axis=-1)[:, low]
        write_stats(logs[:, high], powers[:, high], send_ref, heads)


def merge(mine, theirs, heads, out_shapes, last):
    return pl.pallas_call(
        functools.partial(merge_kernel, heads, last),
        out_shape=out_shapes,
        compiler_params=pltpu.CompilerParams(vmem_limit_bytes=VMEM_LIMIT),
        name="merge",
    )(mine, theirs)


def place_kernel(heads, axis, names, *refs):
    part_refs, (out_ref, logs_ref) = refs[:-2], refs[-2:]
    here = lax.axis_index(axis) if len(part_refs) > 1 else 0
    pieces = []
    if len(part_refs) > 1:
        for k, part_ref in zip(names, part_refs):
            outs, logs = decode(heads, part_ref)
            at = lax.bitwise_xor(here, k)
            out_ref[:, pl.ds(pl.multiple_of(at * heads * DH, DH), heads * DH)] = jnp.concatenate(
                outs, axis=-1
            )
            pieces.append((at, logs))
        columns = []
        for z in range(len(part_refs)):
            columns.append(sum(jnp.where(at == z, logs, 0.0) for at, logs in pieces))
    else:
        outs, logs = decode(heads, part_refs[0])
        for z in range(logs.shape[0]):
            for h in range(heads):
                first = (z * heads + h) * DH
                out_ref[:, first : first + DH] = outs[h][z]
        columns = [logs[z] for z in range(logs.shape[0])]
    logs_ref[...] = jnp.concatenate(columns, axis=-1) * math.log(2.0)


def place(parts, heads, axis, share, names):
    return pl.pallas_call(
        functools.partial(place_kernel, heads, axis, names),
        out_shape=[
            jax.ShapeDtypeStruct((share, HEADS * DH), jnp.float32),
            jax.ShapeDtypeStruct((share, HEADS), jnp.float32),
        ],
        compiler_params=pltpu.CompilerParams(vmem_limit_bytes=VMEM_LIMIT),
        name="place",
    )(*parts)


def across(value, axis, size, bit):
    return lax.ppermute(value, axis, [(i, i ^ bit) for i in range(size)])


def page_limits(page_lists, page_counts, pool, width):
    slots = jnp.arange(page_lists.shape[1], dtype=jnp.int32)
    pages = jnp.arange(pool, dtype=jnp.int32)
    live = jnp.any(
        (page_lists[0][None, :] == pages[:, None]) & (slots < page_counts[0])[None, :], axis=1
    )
    return jnp.broadcast_to(jnp.where(live, -lowest, lowest)[:, None], (pool, width))


def on_device(queries, keys, values, page_lists, page_counts):
    n_head = lax.axis_size("head")
    n_cache = lax.axis_size("cache")
    heads = keys.shape[2] // DH
    share = queries.shape[0] // n_cache
    bits = [1 << i for i in range(n_cache.bit_length() - 1)]
    direct = n_head <= MOST_PERMUTES
    head_at, cache_at = lax.axis_index("head"), lax.axis_index("cache")
    order = [0]
    for bit in reversed(bits):
        order = order + [share_at ^ bit for share_at in order]

    def pick(names, k):
        width = heads * DH
        at = (head_at ^ k) * width
        pieces = [
            lax.dynamic_slice(queries, ((cache_at ^ name) * share, at), (share, width))
            for name in names
        ]
        return jnp.concatenate(pieces)

    half = n_cache // 2
    rows = half * share
    if direct:
        parts = [across(pick(order[:half], k), "head", n_head, k) for k in range(1, n_head)]
        swapped = [across(part, "cache", n_cache, 1) for part in parts]
        q_parts = [pick(order[:half], 0)] + parts + [pick(order[half:], 0)] + swapped
    else:
        shares = queries.reshape(n_cache, share, HEADS * DH)
        same = jnp.concatenate(
            [lax.dynamic_index_in_dim(shares, cache_at ^ name, 0, False) for name in order[:half]]
        )
        moved = lax.all_to_all(
            same.reshape(rows, n_head, heads * DH), "head", split_axis=1, concat_axis=0, tiled=True
        ).reshape(n_head * rows, heads * DH)
        q_parts = [moved, across(moved, "cache", n_cache, 1)]
    all_tok = n_head * queries.shape[0]
    limits = page_limits(page_lists, page_counts, keys.shape[0], min(all_tok, TOK_TILE))
    groups = [range(n_head // 2), range(n_head // 2, n_head)] if direct else [range(n_head)]
    starts = [group[0] * rows for group in groups]
    starts = starts + [n_head * rows + first for first in starts]
    states = attend(q_parts, keys, values, limits, starts)
    width = states[0].shape[1]
    states = [state.reshape(-1, rows, width) for state in states]
    states = list(zip(states[: len(groups)], states[len(groups) :]))[::-1]
    groups = groups[::-1]
    parts = [None] * n_head
    for bit in bits:
        arrived = [across(send, "cache", n_cache, bit) for _, send in states]
        for g, (keep, _) in enumerate(states):
            size, length, _ = keep.shape
            if bit != bits[-1]:
                shapes = [
                    jax.ShapeDtypeStruct((size, length // 2, width), jnp.float32),
                    jax.ShapeDtypeStruct((size, length // 2, width), jnp.int16),
                ]
                states[g] = merge(keep, arrived[g], heads, shapes, False)
            elif direct:
                shapes = [jax.ShapeDtypeStruct((share, width), jnp.int16)] * size
                blocks = merge(keep, arrived[g], heads, shapes, True)
                for k, block in zip(groups[g], blocks):
                    parts[k] = across(block, "head", n_head, k) if k else block
            else:
                shapes = [jax.ShapeDtypeStruct((n_head, share, width), jnp.int16)]
                (blocks,) = merge(keep, arrived[g], heads, shapes, True)
                parts = [lax.all_to_all(blocks, "head", split_axis=0, concat_axis=0, tiled=True)]
    names = list(range(len(parts)))[::-1]
    parts = [parts[k] for k in names]
    return tuple(place(parts, heads, "head", share, names))


def solution(mesh):
    in_specs = (
        P(("group", "head"), None),
        P(("group", "cache"), None, "head"),
        P(("group", "cache"), None, "head"),
        P(("group", "cache"), None),
        P(("group", "cache")),
    )
    out_specs = (P(("group", "head", "cache"), None), P(("group", "head", "cache"), None))
    return jax.shard_map(
        on_device, mesh=mesh, in_specs=in_specs, out_specs=out_specs, check_vma=False
    )
```

```python
import functools
import math

import jax
import jax.numpy as jnp
from jax import lax
from jax.experimental import pallas as pl
from jax.experimental.pallas import tpu as pltpu
from jax.sharding import PartitionSpec as P

HEADS = 32
DH = 128
PAGE = 128
LANES = 128
TOK_TILE = 256
GROUP = 16
MOST_PERMUTES = 8
VMEM_LIMIT = 50 * 2**20

lowest = -1e30
to_log2 = math.log2(math.e) / math.sqrt(DH)


def attend_kernel(n_parts, starts, limits_ref, *refs):
    q_refs = refs[:n_parts]
    k_hbm, v_hbm, k_first, v_first = refs[n_parts : n_parts + 4]
    out_refs = refs[n_parts + 4 : n_parts + 4 + len(starts)]
    q_turned, k_pool, v_pool, stats, k_sem, v_sem = refs[n_parts + 4 + len(starts) :]
    heads, pool = k_pool.shape[:2]
    all_tok = q_turned.shape[2]
    tile = min(all_tok, TOK_TILE)
    tiles = all_tok // tile
    ahead = min(heads, 3)

    def copies(h):
        columns = pl.ds(pl.multiple_of(h * DH, DH), DH)
        return (
            pltpu.make_async_copy(k_hbm.at[:, :, columns], k_pool.at[h], k_sem.at[h]),
            pltpu.make_async_copy(v_hbm.at[:, :, columns], v_pool.at[h], v_sem.at[h]),
        )

    for h in range(1, ahead):
        for copy in copies(h):
            copy.start()
    k_pool[0] = k_first[...]
    v_pool[0] = v_first[...]
    def turn(h):
        lanes = pl.ds(pl.multiple_of(h * DH, DH), DH)
        q_turned[h] = jnp.concatenate([q_ref[:, lanes] for q_ref in q_refs[::-1]], axis=0).T

    for h in range(1 if tiles == 1 else heads):
        turn(h)
    stats[...] = jnp.zeros_like(stats)
    ones = jnp.ones((8, PAGE), jnp.bfloat16)

    def unit(u, carry):
        h, t = u // tiles, lax.rem(u, tiles)

        @pl.when(t == 0)
        def _():
            @pl.when(h > 0)
            def _():
                for copy in copies(h):
                    copy.wait()

            @pl.when(h + ahead < heads)
            def _():
                for copy in copies(h + ahead):
                    copy.start()

        start = pl.multiple_of(t * tile, tile)
        columns = pl.ds(start, tile)
        q_tile = q_turned[h, :, columns]
        if tiles == 1:
            turn(jnp.minimum(h + 1, heads - 1))
        scores, tops = [], []
        for i in range(0, pool, GROUP):
            block = k_pool[h, i : i + GROUP].reshape(GROUP * PAGE, DH)
            both = jnp.dot(block, q_tile, preferred_element_type=jnp.float32)
            for j in range(GROUP):
                scores.append(both[j * PAGE : (j + 1) * PAGE])
                tops.append(jnp.max(scores[-1], axis=0, keepdims=True))
        used = [jnp.minimum(tops[i], limits_ref[i : i + 1, :]) for i in range(pool)]
        best = functools.reduce(jnp.maximum, used)
        total, accum = 0.0, 0.0
        for i in range(pool):
            weights = jnp.exp2((scores[i] - tops[i]) * to_log2).astype(jnp.bfloat16)
            page_out = jnp.dot(
                jnp.concatenate([v_pool[h, i].T, ones], axis=0),
                weights,
                preferred_element_type=jnp.float32,
            )
            fresh = jnp.exp2((used[i] - best) * to_log2)
            total = total + fresh * page_out[DH : DH + 1]
            accum = accum + fresh * page_out[:DH]
        out = accum * (1.0 / total)
        stats[pl.ds(h, 1), columns] = best * to_log2 + jnp.log2(total)
        stats[pl.ds(heads + h, 1), columns] = jnp.max(jnp.abs(out), axis=0, keepdims=True)
        out = out.T
        lanes = pl.ds(pl.multiple_of(h * DH, DH), DH)
        for first, out_ref in zip(starts, out_refs):
            length = out_ref.shape[0]
            if tiles == 1:
                out_ref[:, lanes] = out[first : first + length]
            else:

                @pl.when((start >= first) & (start < first + length))
                def _():
                    out_ref[pl.ds(pl.multiple_of(start - first, tile), tile), lanes] = out

        return carry

    lax.fori_loop(0, heads * tiles, unit, 0)
    for t in range(tiles):
        turned = stats[:, t * tile : (t + 1) * tile].T
        for first, out_ref in zip(starts, out_refs):
            low = max(first, t * tile)
            high = min(first + out_ref.shape[0], (t + 1) * tile)
            if low < high:
                out_ref[low - first : high - first, heads * DH :] = turned[
                    low - t * tile : high - t * tile
                ]


def first_kernel(k_hbm, v_hbm, k_ref, v_ref, sems):
    copies = [
        pltpu.make_async_copy(k_hbm.at[:, :, :DH], k_ref, sems.at[0]),
        pltpu.make_async_copy(v_hbm.at[:, :, :DH], v_ref, sems.at[1]),
    ]
    for copy in copies:
        copy.start()
    for copy in copies:
        copy.wait()


def first_head(keys, values):
    out = jax.ShapeDtypeStruct(keys.shape[:2] + (DH,), keys.dtype)
    return pl.pallas_call(
        first_kernel,
        in_specs=[pl.BlockSpec(memory_space=pl.ANY)] * 2,
        out_specs=[pl.BlockSpec(memory_space=pltpu.VMEM)] * 2,
        scratch_shapes=[pltpu.SemaphoreType.DMA((2,))],
        out_shape=[out, out],
        compiler_params=pltpu.CompilerParams(vmem_limit_bytes=VMEM_LIMIT),
        name="first_head",
    )(keys, values)


def attend(q_parts, keys, values, limits, starts):
    all_tok = sum(part.shape[0] for part in q_parts)
    pool = keys.shape[0]
    heads = keys.shape[2] // DH
    in_vmem = pl.BlockSpec(memory_space=pltpu.VMEM)
    anywhere = pl.BlockSpec(memory_space=pl.ANY)
    outs = [
        jax.ShapeDtypeStruct((end - first, heads * DH + LANES), jnp.float32)
        for first, end in zip(starts, starts[1:] + [all_tok])
    ]
    return pl.pallas_call(
        functools.partial(attend_kernel, len(q_parts), starts),
        in_specs=[in_vmem] * (1 + len(q_parts)) + [anywhere, anywhere, in_vmem, in_vmem],
        out_specs=[in_vmem] * len(outs),
        scratch_shapes=[
            pltpu.VMEM((heads, DH, all_tok), jnp.bfloat16),
            pltpu.VMEM((heads, pool, PAGE, DH), jnp.bfloat16),
            pltpu.VMEM((heads, pool, PAGE, DH), jnp.bfloat16),
            pltpu.VMEM((LANES, all_tok), jnp.float32),
            pltpu.SemaphoreType.DMA((heads,)),
            pltpu.SemaphoreType.DMA((heads,)),
        ],
        out_shape=outs,
        compiler_params=pltpu.CompilerParams(vmem_limit_bytes=VMEM_LIMIT),
        name="attend",
    )(limits, *q_parts[::-1], keys, values, *first_head(keys, values))


def rounded(x):
    return jnp.where(x < 0, x - 0.5, x + 0.5).astype(jnp.int32)


def write_stats(logs, powers, out_ref, heads):
    fixed = rounded(logs * 2.0**19)
    high = lax.shift_right_arithmetic(fixed, 16)
    low = lax.bitwise_and(fixed, 65535) - 32768
    pad = jnp.zeros(logs.shape[:-1] + (LANES - 3 * heads,), jnp.int32)
    stat = jnp.concatenate([high, low, powers.astype(jnp.int32), pad], axis=-1)
    where = (slice(None),) * (len(out_ref.shape) - 1)
    out_ref[where + (slice(heads * DH, heads * DH + LANES),)] = stat.astype(jnp.int16)


def decode(heads, ref):
    where = (slice(None),) * (len(ref.shape) - 1)
    stat = ref[where + (slice(heads * DH, heads * DH + LANES),)].astype(jnp.int32)
    fixed = lax.shift_left(stat[..., :heads], 16) + (stat[..., heads : 2 * heads] + 32768)
    logs = fixed.astype(jnp.float32) * 2.0**-19
    steps = jnp.exp2(stat[..., 2 * heads : 3 * heads].astype(jnp.float32)) * (1.0 / 32767.0)
    outs = []
    for h in range(heads):
        coded = ref[where + (slice(h * DH, (h + 1) * DH),)].astype(jnp.int32).astype(jnp.float32)
        outs.append(coded * steps[..., h : h + 1])
    return outs, logs


def merge_kernel(heads, last, mine_ref, theirs_ref, *out_refs):
    def lanes(h):
        return slice(h * DH, (h + 1) * DH)

    first_stat = heads * DH
    mine_logs = mine_ref[:, :, first_stat : first_stat + heads]
    mine_bound = mine_ref[:, :, first_stat + heads : first_stat + 2 * heads]
    coded = theirs_ref.dtype == jnp.int16
    if coded:
        stat = theirs_ref[:, :, first_stat:].astype(jnp.int32)
        fixed = lax.shift_left(stat[..., :heads], 16) + (stat[..., heads : 2 * heads] + 32768)
        their_logs = fixed.astype(jnp.float32) * 2.0**-19
        their_bound = jnp.exp2(stat[..., 2 * heads : 3 * heads].astype(jnp.float32))
    else:
        their_logs = theirs_ref[:, :, first_stat : first_stat + heads]
        their_bound = theirs_ref[:, :, first_stat + heads : first_stat + 2 * heads]
    top = jnp.maximum(mine_logs, their_logs)
    first, second = jnp.exp2(mine_logs - top), jnp.exp2(their_logs - top)
    both = first + second
    first, second, logs = first / both, second / both, top + jnp.log2(both)
    bound = first * mine_bound + second * their_bound
    powers = jnp.ceil(jnp.log2(jnp.maximum(bound, 2.0**-100)) + 0.001)
    scale = jnp.exp2(-powers) * 32767.0
    if coded:
        second = second * their_bound * (1.0 / 32767.0)
    first_coded, second_coded = first * scale, second * scale

    def joined(h, a, b, rows):
        if coded:
            theirs = theirs_ref[:, :, lanes(h)].astype(jnp.int32).astype(jnp.float32)[:, rows]
        else:
            theirs = theirs_ref[:, rows, lanes(h)]
        return mine_ref[:, rows, lanes(h)] * a[:, rows, h : h + 1] + theirs * b[:, rows, h : h + 1]

    if last:
        everything = slice(0, mine_ref.shape[1])
        for h in range(heads):
            out = rounded(joined(h, first_coded, second_coded, everything)).astype(jnp.int16)
            if len(out_refs[0].shape) == 3:
                out_refs[0][:, :, lanes(h)] = out
            else:
                for block, out_ref in enumerate(out_refs):
                    out_ref[:, lanes(h)] = out[block]
        if len(out_refs[0].shape) == 3:
            write_stats(logs, powers, out_refs[0], heads)
        else:
            for block, out_ref in enumerate(out_refs):
                write_stats(logs[block], powers[block], out_ref, heads)
    else:
        keep_ref, send_ref = out_refs
        half = keep_ref.shape[1]
        low, high = slice(0, half), slice(half, 2 * half)
        for h in range(heads):
            keep_ref[:, :, lanes(h)] = joined(h, first, second, low)
            out = rounded(joined(h, first_coded, second_coded, high))
            send_ref[:, :, lanes(h)] = out.astype(jnp.int16)
        pad = jnp.zeros(logs.shape[:-1] + (LANES - 2 * heads,), jnp.float32)
        keep_ref[:, :, first_stat:] = jnp.concatenate([logs, bound, pad], axis=-1)[:, low]
        write_stats(logs[:, high], powers[:, high], send_ref, heads)


def merge(mine, theirs, heads, out_shapes, last):
    return pl.pallas_call(
        functools.partial(merge_kernel, heads, last),
        out_shape=out_shapes,
        compiler_params=pltpu.CompilerParams(vmem_limit_bytes=VMEM_LIMIT),
        name="merge",
    )(mine, theirs)


def place_kernel(heads, axis, names, *refs):
    part_refs, (out_ref, logs_ref) = refs[:-2], refs[-2:]
    here = lax.axis_index(axis) if len(part_refs) > 1 else 0
    pieces = []
    if len(part_refs) > 1:
        for k, part_ref in zip(names, part_refs):
            outs, logs = decode(heads, part_ref)
            at = lax.bitwise_xor(here, k)
            out_ref[:, pl.ds(pl.multiple_of(at * heads * DH, DH), heads * DH)] = jnp.concatenate(
                outs, axis=-1
            )
            pieces.append((at, logs))
        columns = []
        for z in range(len(part_refs)):
            columns.append(sum(jnp.where(at == z, logs, 0.0) for at, logs in pieces))
    else:
        outs, logs = decode(heads, part_refs[0])
        for z in range(logs.shape[0]):
            for h in range(heads):
                first = (z * heads + h) * DH
                out_ref[:, first : first + DH] = outs[h][z]
        columns = [logs[z] for z in range(logs.shape[0])]
    logs_ref[...] = jnp.concatenate(columns, axis=-1) * math.log(2.0)


def place(parts, heads, axis, share, names):
    return pl.pallas_call(
        functools.partial(place_kernel, heads, axis, names),
        out_shape=[
            jax.ShapeDtypeStruct((share, HEADS * DH), jnp.float32),
            jax.ShapeDtypeStruct((share, HEADS), jnp.float32),
        ],
        compiler_params=pltpu.CompilerParams(vmem_limit_bytes=VMEM_LIMIT),
        name="place",
    )(*parts)


def across(value, axis, size, bit):
    return lax.ppermute(value, axis, [(i, i ^ bit) for i in range(size)])


def page_limits(page_lists, page_counts, pool, width):
    slots = jnp.arange(page_lists.shape[1], dtype=jnp.int32)
    pages = jnp.arange(pool, dtype=jnp.int32)
    live = jnp.any(
        (page_lists[0][None, :] == pages[:, None]) & (slots < page_counts[0])[None, :], axis=1
    )
    return jnp.broadcast_to(jnp.where(live, -lowest, lowest)[:, None], (pool, width))


def on_device(queries, keys, values, page_lists, page_counts):
    n_head = lax.axis_size("head")
    n_cache = lax.axis_size("cache")
    heads = keys.shape[2] // DH
    share = queries.shape[0] // n_cache
    bits = [1 << i for i in range(n_cache.bit_length() - 1)]
    direct = n_head <= MOST_PERMUTES
    head_at, cache_at = lax.axis_index("head"), lax.axis_index("cache")
    order = [0]
    for bit in reversed(bits):
        order = order + [share_at ^ bit for share_at in order]

    def pick(names, k):
        width = heads * DH
        at = (head_at ^ k) * width
        pieces = [
            lax.dynamic_slice(queries, ((cache_at ^ name) * share, at), (share, width))
            for name in names
        ]
        return jnp.concatenate(pieces)

    half = n_cache // 2
    rows = half * share
    if direct:
        parts = [across(pick(order[:half], k), "head", n_head, k) for k in range(1, n_head)]
        swapped = [across(part, "cache", n_cache, 1) for part in parts]
        q_parts = [pick(order[:half], 0)] + parts + [pick(order[half:], 0)] + swapped
    else:
        shares = queries.reshape(n_cache, share, HEADS * DH)
        same = jnp.concatenate(
            [lax.dynamic_index_in_dim(shares, cache_at ^ name, 0, False) for name in order[:half]]
        )
        moved = lax.all_to_all(
            same.reshape(rows, n_head, heads * DH), "head", split_axis=1, concat_axis=0, tiled=True
        ).reshape(n_head * rows, heads * DH)
        q_parts = [moved, across(moved, "cache", n_cache, 1)]
    all_tok = n_head * queries.shape[0]
    limits = page_limits(page_lists, page_counts, keys.shape[0], min(all_tok, TOK_TILE))
    groups = [range(n_head // 2), range(n_head // 2, n_head)] if direct else [range(n_head)]
    starts = [group[0] * rows for group in groups]
    starts = starts + [n_head * rows + first for first in starts]
    states = attend(q_parts, keys, values, limits, starts)
    width = states[0].shape[1]
    states = [state.reshape(-1, rows, width) for state in states]
    states = list(zip(states[: len(groups)], states[len(groups) :]))[::-1]
    groups = groups[::-1]
    parts = [None] * n_head
    for bit in bits:
        arrived = [across(send, "cache", n_cache, bit) for _, send in states]
        for g, (keep, _) in enumerate(states):
            size, length, _ = keep.shape
            if bit != bits[-1]:
                shapes = [
                    jax.ShapeDtypeStruct((size, length // 2, width), jnp.float32),
                    jax.ShapeDtypeStruct((size, length // 2, width), jnp.int16),
                ]
                states[g] = merge(keep, arrived[g], heads, shapes, False)
            elif direct:
                shapes = [jax.ShapeDtypeStruct((share, width), jnp.int16)] * size
                blocks = merge(keep, arrived[g], heads, shapes, True)
                for k, block in zip(groups[g], blocks):
                    parts[k] = across(block, "head", n_head, k) if k else block
            else:
                shapes = [jax.ShapeDtypeStruct((n_head, share, width), jnp.int16)]
                (blocks,) = merge(keep, arrived[g], heads, shapes, True)
                parts = [lax.all_to_all(blocks, "head", split_axis=0, concat_axis=0, tiled=True)]
    names = list(range(len(parts)))[::-1]
    parts = [parts[k] for k in names]
    return tuple(place(parts, heads, "head", share, names))


def solution(mesh):
    in_specs = (
        P(("group", "head"), None),
        P(("group", "cache"), None, "head"),
        P(("group", "cache"), None, "head"),
        P(("group", "cache"), None),
        P(("group", "cache")),
    )
    out_specs = (P(("group", "head", "cache"), None), P(("group", "head", "cache"), None))
    return jax.shard_map(
        on_device, mesh=mesh, in_specs=in_specs, out_specs=out_specs, check_vma=False
    )
```
